32 devices in a mesh: task: 2 (over y), fsdp: 8 (over z, x), view: 2 (over core).
Axes of the slice: x: 2, y: 2, z: 4, core: 2. Of those that a mesh axis runs over, the one named last changes fastest.
Arguments:
- train_input: bfloat16 [4, 2048, 8192], P(('task', 'view'), 'fsdp'), parts along dimension 0, may hold values from -6 to 6
- train_query: bfloat16 [4, 2048, 4096], P(('task', 'view'), 'fsdp'), parts along dimension 0, may hold values from -120 to 120, as said below
- train_keys: bfloat16 [4, 2048, 512], P(('task', 'view'), 'fsdp'), parts along dimension 0, may hold values from -6 to 6, as said below
- train_target: bfloat16 [4, 2048, 4096], P(('task', 'view'), 'fsdp'), parts along dimension 0, may hold values from -6 to 6
- train_segments: int32 [4, 8, 256], P(('task', 'view'), 'fsdp'), parts along dimension 0, may hold values from 0 to 7, never falling along the last dimension, each value on 1 to 64 neighbouring positions
- value_weight: bfloat16 [8192, 512], P('fsdp'), may hold values from -0.0625 to 0.0625
- adapter_down: float32 [16384, 64], P(('task', 'fsdp')), parts along dimension 0, may hold values from -0.0625 to 0.0625
- adapter_up: float32 [128, 512], P('task'), parts along dimension 0, may hold values from -0.75 to 0.75
- score_input: bfloat16 [4, 512, 8192], P(('task', 'view'), 'fsdp'), parts along dimension 0, may hold values from -6 to 6
- score_query: bfloat16 [4, 512, 4096], P(('task', 'view'), 'fsdp'), parts along dimension 0, may hold values from -120 to 120, as said below
- score_keys: bfloat16 [4, 512, 512], P(('task', 'view'), 'fsdp'), parts along dimension 0, may hold values from -6 to 6, as said below
- score_segments: int32 [4, 8, 64], P(('task', 'view'), 'fsdp'), parts along dimension 0, may hold values from 0 to 3, never falling along the last dimension, each value on 1 to 32 neighbouring positions
Outputs:
- new_down: float32 [16384, 64], P(('task', 'fsdp')), parts along dimension 0
- new_up: float32 [128, 512], P('task'), parts along dimension 0
- scored: bfloat16 [4, 512, 4096], P(('task', 'view'), 'fsdp'), parts along dimension 0
The draws below stay inside these ranges and needn't reach their ends.
There are 2 independent parts, one for each index of `task`. The reference program is written for one: setup_inputs(seed, part) draws one part's arguments, and reference() takes and returns one part's arrays. A program takes and returns all parts, laid end to end along the dimension named above; an argument that names none is the same for every part. Nothing has to cross between parts.
Inputs may be any that keep to these rules, and one draw needn't show every extreme that they name: `train_query`: query features of each token. `train_keys`: key features of each token. `score_query`: query features of each token. `score_keys`: key features of each token. `train_segments`: ids never decrease along a packed row. `score_segments`: ids never decrease along a packed row.
All inputs are finite; a program needn't handle non-finite values.
Results may differ from the reference program's by a relative error of at most 0.01.
Values may be sent and summed in bfloat16 or wider, within the bound.
A program may use at most 128 MiB of HBM per device.

```python
import math
import jax
import jax.numpy as jnp
import numpy as np
from jax import lax

D = 8192
Q_HEADS = 32
KV_HEADS = 4
HEAD_DIM = 128
RANK = 64
SEGMENTS = 8
TOK_DEV = 256
SCORE_DEV = 64
VIEWS = 2
GROUP = 8
VALUE_WIDTH = 512
TOKENS = 2048
STOKENS = 512
N_FSDP = 8


def pair_draw(key, rows):
    key_query, key_keys = jax.random.split(key, 2)
    queries = jnp.clip(jax.random.normal(key_query, (VIEWS, rows, Q_HEADS * HEAD_DIM), jnp.float32), -6.0, 6.0)
    keys_all = jnp.clip(jax.random.normal(key_keys, (VIEWS, rows, KV_HEADS * HEAD_DIM), jnp.float32), -6.0, 6.0)
    return (queries, keys_all)


def draw_train_query(key, part):
    return pair_draw(jax.random.fold_in(key, 11), TOKENS)[0].astype(jnp.bfloat16)


def draw_train_keys(key, part):
    return pair_draw(jax.random.fold_in(key, 11), TOKENS)[1].astype(jnp.bfloat16)


def draw_score_query(key, part):
    return pair_draw(jax.random.fold_in(key, 23), STOKENS)[0].astype(jnp.bfloat16)


def draw_score_keys(key, part):
    return pair_draw(jax.random.fold_in(key, 23), STOKENS)[1].astype(jnp.bfloat16)


def with_spikes(entries, rng, source, target, shards_of, factor):
    def block_of(axis_at):
        return (jnp.arange(entries.shape[axis_at]) // (entries.shape[axis_at] // shards_of)).reshape((-1,) + (1,) * (entries.ndim - 1 - axis_at))

    first = jax.random.permutation(rng, shards_of)[block_of(target)]
    other_side = (block_of(target) + shards_of // 2) % shards_of
    return jnp.where((block_of(source) == first) | (block_of(source) == other_side), factor * entries, entries)


def block_levels(rng, extent, cuts, low, largest):
    gain = 1.0
    for position, shards_of in cuts:
        draws = jax.random.uniform(jax.random.fold_in(jax.random.fold_in(rng, 6), position), (shards_of,), jnp.float32, low / len(cuts), largest / len(cuts))
        gain = gain * jnp.repeat(jnp.exp(draws), extent[position] // shards_of).reshape((-1,) + (1,) * (len(extent) - 1 - position))
    return gain


def length_profile(number_of, total, bound, slope):
    loads = [(1 << 20) // math.isqrt(rank ** slope) + 1 for rank in range(2, number_of + 1)]
    rest, holding = total - bound - (number_of - 1), [1] * (number_of - 1)
    while rest > 0:
        free = [i for i in range(number_of - 1) if holding[i] < bound]
        mass, remaining = sum([loads[i] for i in free]), rest
        for i in free:
            extra = min(bound - holding[i], max(1, remaining * loads[i] // mass), rest)
            holding[i] = holding[i] + extra
            rest = rest - extra
    return np.array([bound] + holding)


def uneven_parts(stream_key, count, total, limit, skew):
    if count == 2:
        one = jax.random.randint(stream_key, (), max(1, total - limit), min(limit, total - 1) + 1)
        return jnp.stack([one, total - one])
    sizes = jnp.asarray(length_profile(count, total, limit, skew), jnp.int32)
    couples = (count - 1) // 2
    source_of, receiver = sizes[1:1 + 2 * couples:2], sizes[2:2 + 2 * couples:2]
    room = jnp.minimum(source_of - 1, limit - receiver)
    shifted = jax.random.randint(jax.random.fold_in(stream_key, 1), (couples,), 0, 1 << 20) % (room + 1)
    sizes = sizes.at[1:1 + 2 * couples:2].set(source_of - shifted).at[2:2 + 2 * couples:2].set(receiver + shifted)
    return sizes[jax.random.permutation(jax.random.fold_in(stream_key, 2), count)]


def normal_values(stream_key, extent, scale, bound, cuts=(), kind=jnp.bfloat16):
    factor_of = block_levels(stream_key, extent, cuts, -0.22, 0.18) if cuts else 1.0
    entries = jax.random.normal(stream_key, extent, jnp.float32) * scale * factor_of
    return jnp.minimum(jnp.maximum(entries, -bound), bound).astype(kind)


def heavy_noise(own_key, shape, width, limit, cuts, heavy, held_as=jnp.bfloat16):
    entries = width * jax.random.normal(own_key, shape, jnp.float32)
    if cuts:
        entries = entries * block_levels(own_key, shape, cuts, -0.22, 0.18)
    return jnp.clip(with_spikes(entries, jax.random.fold_in(own_key, 3), *heavy), -limit, limit).astype(held_as)


def setup_inputs(seed: int = 0, part: int = 0) -> dict:
    seeds = jax.random.split(jax.random.key(seed), 13)
    part_splits = jax.random.split(jax.random.fold_in(seeds[12], part), 13)
    return {
        "train_input": heavy_noise(part_splits[0], (VIEWS, TOKENS, D), 1.0, 6.0, ((0, 2), (1, 8)), (1, 2, 8, 2.0)),
        "train_query": draw_train_query(jax.random.fold_in(jax.random.fold_in(seeds[12], part), 71), part),
        "train_keys": draw_train_keys(jax.random.fold_in(jax.random.fold_in(seeds[12], part), 71), part),
        "train_target": normal_values(part_splits[3], (VIEWS, TOKENS, Q_HEADS * HEAD_DIM), 1.0, 6.0, ((0, 2), (1, 8))),
        "train_segments": jax.vmap(lambda own: jnp.searchsorted(jnp.cumsum(uneven_parts(own, SEGMENTS, TOK_DEV, TOK_DEV // 4, 2)), jnp.arange(TOK_DEV), side="right"))(jax.random.split(part_splits[4], VIEWS * N_FSDP)).reshape((VIEWS, N_FSDP, TOK_DEV)).astype(jnp.int32),
        "value_weight": normal_values(seeds[5], (D, VALUE_WIDTH), D ** -0.5, 0.0625, ((0, 8),)),
        "adapter_down": normal_values(part_splits[6], (D, RANK), D ** -0.5, 0.0625, ((0, 8),), jnp.float32),
        "adapter_up": normal_values(part_splits[7], (RANK, VALUE_WIDTH), RANK ** -0.5, 0.75, (), jnp.float32),
        "score_input": normal_values(part_splits[8], (VIEWS, STOKENS, D), 1.0, 6.0, ((0, 2), (1, 8))),
        "score_query": draw_score_query(jax.random.fold_in(jax.random.fold_in(seeds[12], part), 71), part),
        "score_keys": draw_score_keys(jax.random.fold_in(jax.random.fold_in(seeds[12], part), 71), part),
        "score_segments": jax.vmap(lambda own: jnp.searchsorted(jnp.cumsum(uneven_parts(own, 4, SCORE_DEV, SCORE_DEV // 2, 1)), jnp.arange(SCORE_DEV), side="right"))(jax.random.split(part_splits[11], VIEWS * N_FSDP)).reshape((VIEWS, N_FSDP, SCORE_DEV)).astype(jnp.int32),
    }


adapter_scale_factor = 0.5
rate_down = 2e-05
rate_up = 0.001

def attend_row(query, keyset, value_rows, segment):
    length = query.shape[0]
    query_heads = query.reshape(length, KV_HEADS, GROUP, HEAD_DIM).astype(jnp.float32)
    key_heads = keyset.reshape(length, KV_HEADS, HEAD_DIM).astype(jnp.float32)
    logits = jnp.einsum('qgjd,kgd->gjqk', query_heads, key_heads) * HEAD_DIM ** (-0.5)
    positions = jnp.arange(length, dtype=jnp.int32)
    allowed = (positions[None, :] <= positions[:, None]) & (segment[:, None] == segment[None, :])
    logits = jnp.where(allowed, logits, -1e+30)
    peak = lax.optimization_barrier(jnp.max(logits, axis=-1, keepdims=True))
    weights = jnp.exp(logits - peak)
    probs = (weights / lax.optimization_barrier(jnp.sum(weights, axis=-1, keepdims=True))).astype(jnp.bfloat16)
    value_heads = value_rows.reshape(length, KV_HEADS, HEAD_DIM).astype(jnp.float32)
    attended = jnp.einsum('gjqk,kgd->qgjd', probs.astype(jnp.float32), value_heads)
    return (probs, attended.reshape(length, Q_HEADS * HEAD_DIM))

def values_grad(probs, d_out):
    length = d_out.shape[0]
    heads = d_out.reshape(length, KV_HEADS, GROUP, HEAD_DIM).astype(jnp.float32)
    summed = jnp.einsum('gjqk,qgjd->kgd', probs.astype(jnp.float32), heads)
    return summed.reshape(length, VALUE_WIDTH).astype(jnp.bfloat16)

def project(rows_in, value_weight, down_half, upper_weight_half):
    lower_rank_half = jnp.dot(rows_in, down_half, preferred_element_type=jnp.float32).astype(jnp.bfloat16)
    frozen_base_weight = jnp.dot(rows_in, value_weight, preferred_element_type=jnp.float32)
    value_rows = (frozen_base_weight + adapter_scale_factor * jnp.dot(lower_rank_half, upper_weight_half, preferred_element_type=jnp.float32)).astype(jnp.bfloat16)
    return (value_rows, lower_rank_half)

def reference(train_input, train_query, train_keys, train_target, train_segments, value_weight, adapter_down, adapter_up, score_input, score_query, score_keys, score_segments):
    down_half = adapter_down.astype(jnp.bfloat16)
    upper_weight_half = adapter_up.astype(jnp.bfloat16)
    train_rows = train_input.reshape(-1, D)
    value_rows, lower_rank_half = project(train_rows, value_weight, down_half, upper_weight_half)
    count_rows = VIEWS * N_FSDP

    def row_step(pieces):
        query, keyset, vals, segment, goal = pieces
        probs, attended = attend_row(query, keyset, vals, segment)
        d_out = (attended - goal.astype(jnp.float32)).astype(jnp.bfloat16)
        return values_grad(probs, d_out)
    value_output_gradient = lax.map(row_step, (train_query.reshape(count_rows, TOK_DEV, Q_HEADS * HEAD_DIM), train_keys.reshape(count_rows, TOK_DEV, VALUE_WIDTH), value_rows.reshape(count_rows, TOK_DEV, VALUE_WIDTH), train_segments.reshape(count_rows, TOK_DEV), train_target.reshape(count_rows, TOK_DEV, Q_HEADS * HEAD_DIM)))
    value_output_gradient = value_output_gradient.reshape(-1, VALUE_WIDTH)
    low_rank_gradient = (adapter_scale_factor * jnp.dot(value_output_gradient, upper_weight_half.T, preferred_element_type=jnp.float32)).astype(jnp.bfloat16)
    grad_down = jnp.dot(train_rows.T, low_rank_gradient, preferred_element_type=jnp.float32)
    up_weight_gradient = adapter_scale_factor * jnp.dot(lower_rank_half.T, value_output_gradient, preferred_element_type=jnp.float32)
    new_down = adapter_down - rate_down * grad_down
    new_up = adapter_up - rate_up * up_weight_gradient
    score_rows = score_input.reshape(-1, D)
    score_values, score_low = project(score_rows, value_weight, new_down.astype(jnp.bfloat16), new_up.astype(jnp.bfloat16))

    def score_step(pieces):
        query, keyset, vals, segment = pieces
        probs, attended = attend_row(query, keyset, vals, segment)
        return attended.astype(jnp.bfloat16)
    scored = lax.map(score_step, (score_query.reshape(count_rows, SCORE_DEV, Q_HEADS * HEAD_DIM), score_keys.reshape(count_rows, SCORE_DEV, VALUE_WIDTH), score_values.reshape(count_rows, SCORE_DEV, VALUE_WIDTH), score_segments.reshape(count_rows, SCORE_DEV)))
    return (new_down, new_up, scored.reshape(VIEWS, STOKENS, Q_HEADS * HEAD_DIM))
```

```python
import jax
import jax.numpy as jnp
from jax import lax
from jax.experimental import pallas as pl
from jax.experimental.pallas import tpu as pltpu
from jax.sharding import PartitionSpec as P

Q_HEADS = 32
KV_HEADS = 4
HEAD_DIM = 128
GROUP = 8
VALUE_WIDTH = 512


adapter_scale_factor = 0.5
rate_down = 2e-05
rate_up = 0.001


def attend_row(query, keyset, value_rows, segment):
    length = query.shape[0]
    query_heads = query.reshape(length, KV_HEADS, GROUP, HEAD_DIM)
    key_heads = keyset.reshape(length, KV_HEADS, HEAD_DIM)
    logits = jnp.einsum(
        "qgjd,kgd->gjqk", query_heads, key_heads, preferred_element_type=jnp.float32
    ) * HEAD_DIM ** (-0.5)
    positions = jnp.arange(length, dtype=jnp.int32)
    allowed = (positions[None, :] <= positions[:, None]) & (segment[:, None] == segment[None, :])
    logits = jnp.where(allowed, logits, -1e30)
    peak = jnp.max(logits, axis=-1, keepdims=True)
    weights = jnp.exp(logits - peak)
    probs = (weights / jnp.sum(weights, axis=-1, keepdims=True)).astype(jnp.bfloat16)
    value_heads = value_rows.reshape(length, KV_HEADS, HEAD_DIM)
    attended = jnp.einsum("gjqk,kgd->qgjd", probs, value_heads, preferred_element_type=jnp.float32)
    return (probs, attended.reshape(length, Q_HEADS * HEAD_DIM))


def values_grad(probs, d_out):
    length = d_out.shape[0]
    heads = d_out.reshape(length, KV_HEADS, GROUP, HEAD_DIM)
    summed = jnp.einsum("gjqk,qgjd->kgd", probs, heads, preferred_element_type=jnp.float32)
    return summed.reshape(length, VALUE_WIDTH).astype(jnp.bfloat16)


def add_pieces(rows_in, pieces):
    return (
        jnp.dot(rows_in, pieces[0], preferred_element_type=jnp.float32),
        jnp.dot(rows_in, pieces[1], preferred_element_type=jnp.float32),
    )


def body(
    train_input,
    train_query,
    train_keys,
    train_target,
    train_segments,
    value_weight,
    adapter_down,
    adapter_up,
    score_input,
    score_query,
    score_keys,
    score_segments,
):
    width = train_input.shape[-1]
    value_width = value_weight.shape[1]
    count_rows = train_segments.shape[0] * train_segments.shape[1]
    row_length = train_segments.shape[2]
    score_length = score_segments.shape[2]
    down_half = adapter_down.astype(jnp.bfloat16)
    upper_weight_half = adapter_up.astype(jnp.bfloat16)
    train_rows = train_input.reshape(-1, width)
    frozen_base_weight, low = add_pieces(
        train_rows,
        (
            lax.all_gather(value_weight, "fsdp", axis=0, tiled=True),
            lax.all_gather(down_half, "fsdp", axis=0, tiled=True),
        ),
    )
    lower_rank_half = low.astype(jnp.bfloat16)
    value_rows = (
        frozen_base_weight
        + adapter_scale_factor
        * jnp.dot(lower_rank_half, upper_weight_half, preferred_element_type=jnp.float32)
    ).astype(jnp.bfloat16)
    probs, attended = jax.vmap(attend_row)(
        train_query,
        train_keys,
        value_rows.reshape(count_rows, row_length, -1),
        train_segments.reshape(count_rows, row_length),
    )
    d_out = (attended - train_target.astype(jnp.float32)).astype(jnp.bfloat16)
    value_output_gradient = jax.vmap(values_grad)(probs, d_out).reshape(-1, value_width)
    low_rank_gradient = (
        adapter_scale_factor
        * lax.dot_general(
            value_output_gradient,
            upper_weight_half,
            (((1,), (1,)), ((), ())),
            preferred_element_type=jnp.float32,
        )
    ).astype(jnp.bfloat16)
    local_up_gradient = adapter_scale_factor * lax.dot_general(
        lower_rank_half,
        value_output_gradient,
        (((0,), (0,)), ((), ())),
        preferred_element_type=jnp.float32,
    )
    grad_down = lax.psum_scatter(
        lax.dot_general(
            train_rows,
            low_rank_gradient,
            (((0,), (0,)), ((), ())),
            preferred_element_type=jnp.float32,
        ),
        "fsdp",
        scatter_dimension=0,
        tiled=True,
    )
    grad_down = lax.psum(grad_down, "view")
    up_weight_gradient = lax.psum(local_up_gradient, ("fsdp", "view"))
    new_down = adapter_down - rate_down * grad_down
    new_up = adapter_up - rate_up * up_weight_gradient
    new_down_half = new_down.astype(jnp.bfloat16)
    new_up_half = new_up.astype(jnp.bfloat16)
    score_rows = score_input.reshape(-1, width)
    score_base, score_low = add_pieces(
        score_rows,
        (
            lax.all_gather(value_weight, "fsdp", axis=0, tiled=True),
            lax.all_gather(new_down_half, "fsdp", axis=0, tiled=True),
        ),
    )
    score_values = (
        score_base
        + adapter_scale_factor
        * jnp.dot(score_low.astype(jnp.bfloat16), new_up_half, preferred_element_type=jnp.float32)
    ).astype(jnp.bfloat16)
    score_probs, score_attended = jax.vmap(attend_row)(
        score_query,
        score_keys,
        score_values.reshape(count_rows, score_length, -1),
        score_segments.reshape(count_rows, score_length),
    )
    scored = score_attended.astype(jnp.bfloat16)
    return (new_down, new_up, scored)


F32, BF16 = jnp.float32, jnp.bfloat16
N, DEPTH = 8, 4
BLOCK = 64
WINDOW = 2 * BLOCK
NT = (((1,), (1,)), ((), ()))
TN = (((0,), (0,)), ((), ()))
UP, DOWN, SIDE, TWIN, CORE = range(5)


def nt_dot(a, b):
    return lax.dot_general(a, b, NT, preferred_element_type=F32)


def tn_dot(a, b):
    return lax.dot_general(a, b, TN, preferred_element_type=F32)


def dot(a, b):
    return jnp.dot(a, b, preferred_element_type=F32)


def lanes(start, size):
    return pl.ds(pl.multiple_of(start, size), size)


def stack_heads(ref, rows, g):
    return jnp.concatenate(
        [ref[rows, lanes((g * GROUP + j) * HEAD_DIM, HEAD_DIM)] for j in range(GROUP)], axis=0
    )


def softmax_rows(logits, allowed):
    shape = logits.shape
    logits = (logits * HEAD_DIM ** (-0.5)).reshape(GROUP, BLOCK, shape[-1])
    logits = jnp.where(allowed[None], logits, -1e30)
    weights = jnp.exp(logits - jnp.max(logits, axis=-1, keepdims=True))
    probs = weights * (1.0 / jnp.sum(weights, axis=-1, keepdims=True))
    return probs.reshape(shape).astype(BF16)


def fused_kernel(
    x_hbm, q_hbm, k_hbm, goal_hbm, seg_row, seg_col, w_hbm, down_t, up_ref,
    sx_hbm, sq_hbm, sk_hbm, sseg_row, sseg_col,
    new_down_t, new_up, scored,
    xs, qs, ks, goal, sq, sk, wbuf, dbuf, ndbuf, probs, sprobs, base, vals, dvals,
    low_s, gmine, gsend, gpair, rsend, rrecv, fhalf, frecv, gu, gupair, gusum, gurecv, gupart, guall,
    s_loc, s_w, r_w, s_d, r_d, s_nd, r_nd, s_gp, r_gp, s_rs, r_rs, s_f, r_f,
    s_up, r_up, s_ur, r_ur, s_ua, r_ua, s_uc, r_uc,
):
    t, f, c = lax.axis_index("task"), lax.axis_index("fsdp"), lax.axis_index("view")
    z, x = lax.div(f, 2), lax.rem(f, 2)
    other_t, other_x, other_c = 1 - t, 1 - x, 1 - c
    width = xs.shape[1]
    part = width // N
    half = part // 2
    rows = vals.shape[0]
    late = []

    def device(kind):
        return {
            UP: {"fsdp": f + 2},
            DOWN: {"fsdp": f - 2},
            SIDE: {"fsdp": 2 * z + other_x},
            TWIN: {"task": other_t},
            CORE: {"view": other_c},
        }[kind]

    def exists(kind):
        return {UP: z < DEPTH - 1, DOWN: z > 0}.get(kind, True)

    def start(make, pred=True):
        if pred is True:
            make().start()
        else:
            pl.when(pred)(lambda: make().start())
        late.append((make, pred))

    def send(kind, src, dst, s_sem, r_sem, pred=True):
        where = exists(kind)
        if where is not True:
            pred = where if pred is True else jnp.logical_and(where, pred)

        def make():
            return pltpu.make_async_remote_copy(
                src_ref=src, dst_ref=dst, send_sem=s_sem, recv_sem=r_sem,
                device_id=device(kind), device_id_type=pl.DeviceIdType.MESH,
            )

        start(make, pred)

    def peer_send(peer, src, dst, s_sem, r_sem):
        def make():
            return pltpu.make_async_remote_copy(
                src_ref=src, dst_ref=dst, send_sem=s_sem, recv_sem=r_sem,
                device_id={"fsdp": peer}, device_id_type=pl.DeviceIdType.MESH,
            )

        start(make)

    def arrived(dst, r_sem, pred=True):
        def wait():
            pltpu.make_async_remote_copy(
                src_ref=dst, dst_ref=dst, send_sem=r_sem, recv_sem=r_sem,
                device_id={"view": other_c}, device_id_type=pl.DeviceIdType.MESH,
            ).wait_recv()

        if pred is True:
            wait()
        else:
            pl.when(pred)(wait)

    def peers():
        return [lax.rem(f + k, N) for k in range(1, N)]

    barrier = pltpu.get_barrier_semaphore()
    for peer in peers():
        pl.semaphore_signal(barrier, inc=1, device_id={"fsdp": peer}, device_id_type=pl.DeviceIdType.MESH)
    for kind in (TWIN, CORE):
        pl.semaphore_signal(barrier, inc=1, device_id=device(kind), device_id_type=pl.DeviceIdType.MESH)

    local = [
        (q_hbm, qs),
        (k_hbm, ks),
        (sq_hbm, sq),
        (sk_hbm, sk),
        (x_hbm, xs.at[pl.ds(0, rows)]),
        (sx_hbm, xs.at[pl.ds(rows, BLOCK)]),
        (goal_hbm, goal),
        (w_hbm, wbuf.at[pl.ds(4 * f, 4)]),
    ]
    loads = [pltpu.make_async_copy(a, b, s_loc.at[i]) for i, (a, b) in enumerate(local)]
    for load in loads:
        load.start()
    for side in range(2):
        dbuf[2 * f + side] = down_t[:, side * half:(side + 1) * half].astype(BF16)
    pl.semaphore_wait(barrier, N + 1)

    line = [(d, s, z - s * d) for d in range(1, DEPTH) for s in (1, -1)]

    def inside(zp):
        return jnp.logical_and(zp >= 0, zp < DEPTH)

    def piece_send(buf, s_sem, r_sem, kind, i, pred=True):
        send(kind, buf.at[i], buf.at[i], s_sem.at[kind, i], r_sem.at[i], pred)

    def pieces_own(buf, s_sem, r_sem):
        for kind in (UP, DOWN, SIDE):
            piece_send(buf, s_sem, r_sem, kind, 2 * f + c)

    def pieces_line(buf, s_sem, r_sem, d):
        for dd, s, zp in line:
            if dd == d:
                ok, i = inside(zp), 2 * (2 * zp + x) + c
                arrived(buf.at[i], r_sem.at[i], ok)
                for kind in (UP if s > 0 else DOWN, SIDE, CORE):
                    piece_send(buf, s_sem, r_sem, kind, i, ok)

    def pieces_side(buf, s_sem, r_sem, d):
        for dd, s, zp in [(0, 1, z)] + line:
            if dd == d:
                ok, i = (True if d == 0 else inside(zp)), 2 * (2 * zp + other_x) + c
                arrived(buf.at[i], r_sem.at[i], ok)
                piece_send(buf, s_sem, r_sem, CORE, i, ok)

    def pieces_core(buf, r_sem):
        for peer in peers():
            i = 2 * peer + other_c
            arrived(buf.at[i], r_sem.at[i])

    mine, theirs = 2 * t + c, 2 * other_t + c

    def w_send(kind, i, pred=True):
        send(kind, wbuf.at[i], wbuf.at[i], s_w.at[kind, i], r_w.at[i], pred)

    def w_own():
        for kind, q in ((UP, mine), (DOWN, mine), (SIDE, mine), (SIDE, theirs)):
            i = 4 * f + q
            send(kind, w_hbm.at[q], wbuf.at[i], s_w.at[kind, i], r_w.at[i])

    def w_line(d):
        for dd, s, zp in line:
            if dd == d:
                ok, i = inside(zp), 4 * (2 * zp + x) + mine
                arrived(wbuf.at[i], r_w.at[i], ok)
                for kind in (UP if s > 0 else DOWN, SIDE, TWIN, CORE):
                    w_send(kind, i, ok)

    def w_side(d):
        if d == 0:
            for q in (mine, theirs):
                i = 4 * (2 * z + other_x) + q
                arrived(wbuf.at[i], r_w.at[i])
                w_send(CORE, i)
            return
        for dd, s, zp in line:
            if dd == d:
                ok, i = inside(zp), 4 * (2 * zp + other_x) + mine
                arrived(wbuf.at[i], r_w.at[i], ok)
                w_send(TWIN, i, ok)
                w_send(CORE, i, ok)

    def w_twin(d, xx):
        for dd, s, zp in line:
            if dd == d:
                ok, i = inside(zp), 4 * (2 * zp + xx) + theirs
                arrived(wbuf.at[i], r_w.at[i], ok)
                w_send(CORE, i, ok)

    def train_probs(b):
        first = max(b - 1, 0) * BLOCK
        position_q = b * BLOCK + lax.broadcasted_iota(jnp.int32, (BLOCK, WINDOW), 0)
        position_k = first + lax.broadcasted_iota(jnp.int32, (BLOCK, WINDOW), 1)
        same = seg_col[pl.ds(b * BLOCK, BLOCK), :] == seg_row[b]
        allowed = (position_k <= position_q) & same

        def head_group(g, _):
            q = stack_heads(qs, pl.ds(b * BLOCK, BLOCK), g)
            k = ks[pl.ds(first, WINDOW), lanes(g * HEAD_DIM, HEAD_DIM)]
            probs[b * KV_HEADS + g] = softmax_rows(nt_dot(q, k), allowed)
            return 0

        lax.fori_loop(0, KV_HEADS, head_group, 0)

    def score_probs():
        order_q = lax.broadcasted_iota(jnp.int32, (BLOCK, BLOCK), 0)
        order_k = lax.broadcasted_iota(jnp.int32, (BLOCK, BLOCK), 1)
        allowed = (order_k <= order_q) & (sseg_col[...] == sseg_row[...])

        def head_group(g, _):
            q = stack_heads(sq, pl.ds(0, BLOCK), g)
            sprobs[g] = softmax_rows(nt_dot(q, sk[:, lanes(g * HEAD_DIM, HEAD_DIM)]), allowed)
            return 0

        lax.fori_loop(0, KV_HEADS, head_group, 0)

    dset = (dbuf, s_d, r_d)
    pieces_own(*dset)
    w_own()
    for i in range(4):
        loads[i].wait()
    train_probs(0)
    pieces_line(*dset, 1)
    w_line(1)
    pieces_side(*dset, 0)
    w_side(0)
    train_probs(1)
    pieces_line(*dset, 2)
    w_line(2)
    pieces_side(*dset, 1)
    w_side(1)
    w_twin(1, x)
    train_probs(2)
    pieces_line(*dset, 3)
    w_line(3)
    pieces_side(*dset, 2)
    w_side(2)
    w_twin(2, x)
    w_twin(1, other_x)
    train_probs(3)
    pieces_side(*dset, 3)
    w_side(3)
    w_twin(3, x)
    w_twin(2, other_x)
    score_probs()
    for i in range(4, 8):
        loads[i].wait()
    pieces_core(dbuf, r_d)

    def low_step(i, acc):
        return acc + nt_dot(xs[pl.ds(0, rows), lanes(i * half, half)], dbuf[i])

    low = lax.fori_loop(0, 2 * N, low_step, jnp.zeros((rows, low_s.shape[1]), F32)).astype(BF16)
    low_s[...] = low
    w_twin(3, other_x)
    for peer in peers():
        for q in (2 * t + other_c, 2 * other_t + other_c):
            i = 4 * peer + q
            arrived(wbuf.at[i], r_w.at[i])

    base[...] = jnp.zeros_like(base)

    def base_step(i, _):
        base[...] += dot(xs[:, lanes(i * part, part)], wbuf[pl.ds(4 * i, 4)].reshape(part, VALUE_WIDTH))
        return 0

    lax.fori_loop(0, N, base_step, 0)
    up_half = up_ref[...].astype(BF16)
    vals[...] = (base[pl.ds(0, rows), :] + adapter_scale_factor * dot(low, up_half)).astype(BF16)

    dvals[...] = jnp.zeros_like(dvals)
    for b in range(rows // BLOCK):
        first = max(b - 1, 0) * BLOCK

        def head_group(g, _, b=b, first=first):
            p = probs[b * KV_HEADS + g]
            cols = lanes(g * HEAD_DIM, HEAD_DIM)
            attended = dot(p, vals[pl.ds(first, WINDOW), cols])
            d_out = (attended - stack_heads(goal, pl.ds(b * BLOCK, BLOCK), g).astype(F32)).astype(BF16)
            dvals[pl.ds(first, WINDOW), cols] += tn_dot(p, d_out)
            return 0

        lax.fori_loop(0, KV_HEADS, head_group, 0)
    dv = dvals[...].astype(BF16)
    dlow_t = (adapter_scale_factor * nt_dot(up_half, dv)).astype(BF16)

    def grad_of(peer, side):
        return dot(dlow_t, xs[pl.ds(0, rows), lanes(peer * part + side * half, half)])

    order = peers() + [f]
    for n, peer in enumerate(order):
        gsend[n] = grad_of(peer, other_c).astype(BF16)
        send(CORE, gsend.at[n], gpair.at[n], s_gp.at[n], r_gp.at[n])
    gu[...] = adapter_scale_factor * tn_dot(low_s[...], dv)
    ucols = VALUE_WIDTH // 2
    send(CORE, gu.at[:, lanes(other_c * ucols, ucols)], gupair, s_up, r_up)
    for n, peer in enumerate(order):
        gmine[n] = grad_of(peer, c)
    for n, peer in enumerate(order[:-1]):
        arrived(gpair.at[n], r_gp.at[n])
        rsend[n] = (gmine[n] + gpair[n].astype(F32)).astype(BF16)
        peer_send(peer, rsend.at[n], rrecv.at[n], s_rs.at[n], r_rs.at[n])
    arrived(gupair, r_up)
    gusum[...] = gu[:, lanes(c * ucols, ucols)] + gupair[...]
    urows = gusum.shape[0] // N
    for n, peer in enumerate(order[:-1]):
        peer_send(
            peer, gusum.at[pl.ds(pl.multiple_of(peer * urows, urows), urows)], gurecv.at[n], s_ur.at[n], r_ur.at[n]
        )
    arrived(gpair.at[N - 1], r_gp.at[N - 1])
    total = gmine[N - 1] + gpair[N - 1].astype(F32)
    for n in range(N - 1):
        arrived(rrecv.at[n], r_rs.at[n])
        total = total + rrecv[n].astype(F32)
    new_half = down_t[:, lanes(c * half, half)] - rate_down * total
    fhalf[...] = new_half
    ndbuf[2 * f + c] = new_half.astype(BF16)
    ndset = (ndbuf, s_nd, r_nd)
    pieces_own(*ndset)
    send(CORE, fhalf, frecv, s_f, r_f)

    utotal = gusum[pl.ds(pl.multiple_of(f * urows, urows), urows), :]
    for n in range(N - 1):
        arrived(gurecv.at[n], r_ur.at[n])
        utotal = utotal + gurecv[n]
    gupart[...] = utotal
    guall[c, pl.ds(pl.multiple_of(f * urows, urows), urows), :] = utotal
    for n, peer in enumerate(order[:-1]):
        peer_send(
            peer, gupart, guall.at[c, pl.ds(pl.multiple_of(f * urows, urows), urows)], s_ua.at[n], r_ua.at[f]
        )
    pieces_line(*ndset, 1)
    pieces_side(*ndset, 0)
    pieces_line(*ndset, 2)
    pieces_side(*ndset, 1)
    pieces_line(*ndset, 3)
    for peer in peers():
        arrived(guall.at[c, pl.ds(pl.multiple_of(peer * urows, urows), urows)], r_ua.at[peer])
    send(CORE, guall.at[c], guall.at[c], s_uc, r_uc)
    pieces_side(*ndset, 2)
    pieces_side(*ndset, 3)

    arrived(frecv, r_f)
    new_down_t[:, lanes(c * half, half)] = fhalf[...]
    new_down_t[:, lanes(other_c * half, half)] = frecv[...]
    ndbuf[2 * f + other_c] = frecv[...].astype(BF16)
    arrived(guall.at[other_c], r_uc)
    for side in range(2):
        cols = pl.ds(side * ucols, ucols)
        new_up[:, cols] = up_ref[:, cols] - rate_up * guall[side]
    pieces_core(ndbuf, r_nd)

    def score_low_step(i, acc):
        return acc + nt_dot(xs[pl.ds(rows, BLOCK), lanes(i * half, half)], ndbuf[i])

    slow = lax.fori_loop(0, 2 * N, score_low_step, jnp.zeros((BLOCK, low_s.shape[1]), F32)).astype(BF16)
    svals = (
        base[pl.ds(rows, BLOCK), :] + adapter_scale_factor * dot(slow, new_up[...].astype(BF16))
    ).astype(BF16)
    for g in range(KV_HEADS):
        attended = dot(sprobs[g], svals[:, g * HEAD_DIM:(g + 1) * HEAD_DIM]).astype(BF16)
        for j in range(GROUP):
            at = (g * GROUP + j) * HEAD_DIM
            scored[:, at:at + HEAD_DIM] = attended[j * BLOCK:(j + 1) * BLOCK]

    def finish(make):
        make().wait_send()

    for make, pred in late:
        if pred is True:
            finish(make)
        else:
            pl.when(pred)(lambda make=make: finish(make))


def fused_body(
    train_input, train_query, train_keys, train_target, train_segments, value_weight, adapter_down, adapter_up,
    score_input, score_query, score_keys, score_segments,
):
    rows, width = train_input.shape[1:]
    part, rank = adapter_down.shape
    half = part // 2
    heads = train_query.shape[2]
    srows = score_input.shape[1]
    vw = value_weight.shape[1]
    seg = train_segments.reshape(rows)
    sseg = score_segments.reshape(srows)
    windows = jnp.stack([
        seg[max(b - 1, 0) * BLOCK:max(b - 1, 0) * BLOCK + WINDOW].reshape(1, WINDOW) for b in range(rows // BLOCK)
    ])
    hbm, vmem = pl.BlockSpec(memory_space=pl.ANY), pl.BlockSpec(memory_space=pltpu.VMEM)
    sem = pltpu.SemaphoreType.DMA
    uc, ur = vw // 2, rank // N
    scratch = [
        pltpu.VMEM((rows + srows, width), BF16),
        pltpu.VMEM((rows, heads), BF16),
        pltpu.VMEM((rows, vw), BF16),
        pltpu.VMEM((rows, heads), BF16),
        pltpu.VMEM((srows, heads), BF16),
        pltpu.VMEM((srows, vw), BF16),
        pltpu.VMEM((4 * N, part // 4, vw), BF16),
        pltpu.VMEM((2 * N, rank, half), BF16),
        pltpu.VMEM((2 * N, rank, half), BF16),
        pltpu.VMEM((rows // BLOCK * KV_HEADS, GROUP * BLOCK, WINDOW), BF16),
        pltpu.VMEM((KV_HEADS, GROUP * BLOCK, BLOCK), BF16),
        pltpu.VMEM((rows + srows, vw), F32),
        pltpu.VMEM((rows, vw), BF16),
        pltpu.VMEM((rows, vw), F32),
        pltpu.VMEM((rows, rank), BF16),
        pltpu.VMEM((N, rank, half), F32),
        pltpu.VMEM((N, rank, half), BF16),
        pltpu.VMEM((N, rank, half), BF16),
        pltpu.VMEM((N - 1, rank, half), BF16),
        pltpu.VMEM((N - 1, rank, half), BF16),
        pltpu.VMEM((rank, half), F32),
        pltpu.VMEM((rank, half), F32),
        pltpu.VMEM((rank, vw), F32),
        pltpu.VMEM((rank, uc), F32),
        pltpu.VMEM((rank, uc), F32),
        pltpu.VMEM((N - 1, ur, uc), F32),
        pltpu.VMEM((ur, uc), F32),
        pltpu.VMEM((2, rank, uc), F32),
        sem((8,)),
        sem((5, 4 * N)), sem((4 * N,)),
        sem((5, 2 * N)), sem((2 * N,)),
        sem((5, 2 * N)), sem((2 * N,)),
        sem((N,)), sem((N,)),
        sem((N - 1,)), sem((N - 1,)),
        sem, sem,
        sem, sem,
        sem((N - 1,)), sem((N - 1,)),
        sem((N - 1,)), sem((N,)),
        sem, sem,
    ]
    new_down_t, new_up, scored = pl.pallas_call(
        fused_kernel,
        out_shape=(
            jax.ShapeDtypeStruct((rank, part), F32),
            jax.ShapeDtypeStruct(adapter_up.shape, F32),
            jax.ShapeDtypeStruct((srows, heads), BF16),
        ),
        in_specs=[hbm, hbm, hbm, hbm, vmem, vmem, hbm, vmem, vmem, hbm, hbm, hbm, vmem, vmem],
        out_specs=(vmem, vmem, vmem),
        scratch_shapes=scratch,
        compiler_params=pltpu.CompilerParams(
            collective_id=0, has_side_effects=True, vmem_limit_bytes=52 * 1024 * 1024
        ),
        name="test_time_step",
    )(
        train_input[0], train_query[0], train_keys[0], train_target[0], windows, seg.reshape(rows, 1),
        value_weight.reshape(4, part // 4, vw), adapter_down.T, adapter_up,
        score_input[0], score_query[0], score_keys[0], sseg.reshape(1, srows), sseg.reshape(srows, 1),
    )
    return (new_down_t.T, new_up, scored[None])


def solution(mesh):
    in_specs = (
        P(("task", "view"), "fsdp", None),
        P(("task", "view"), "fsdp", None),
        P(("task", "view"), "fsdp", None),
        P(("task", "view"), "fsdp", None),
        P(("task", "view"), "fsdp", None),
        P("fsdp", None),
        P(("task", "fsdp"), None),
        P("task", None),
        P(("task", "view"), "fsdp", None),
        P(("task", "view"), "fsdp", None),
        P(("task", "view"), "fsdp", None),
        P(("task", "view"), "fsdp", None),
    )
    out_specs = (P(("task", "fsdp"), None), P("task", None), P(("task", "view"), "fsdp", None))
    local = fused_body if (mesh.shape["fsdp"], mesh.shape["view"]) == (8, 2) else body
    return jax.shard_map(local, mesh=mesh, in_specs=in_specs, out_specs=out_specs, check_vma=False)
```

```python
import jax
import jax.numpy as jnp
from jax import lax
from jax.experimental import pallas as pl
from jax.experimental.pallas import tpu as pltpu
from jax.sharding import PartitionSpec as P

Q_HEADS = 32
KV_HEADS = 4
HEAD_DIM = 128
GROUP = 8
VALUE_WIDTH = 512


adapter_scale_factor = 0.5
rate_down = 2e-05
rate_up = 0.001


def attend_row(query, keyset, value_rows, segment):
    length = query.shape[0]
    query_heads = query.reshape(length, KV_HEADS, GROUP, HEAD_DIM)
    key_heads = keyset.reshape(length, KV_HEADS, HEAD_DIM)
    logits = jnp.einsum(
        "qgjd,kgd->gjqk", query_heads, key_heads, preferred_element_type=jnp.float32
    ) * HEAD_DIM ** (-0.5)
    positions = jnp.arange(length, dtype=jnp.int32)
    allowed = (positions[None, :] <= positions[:, None]) & (segment[:, None] == segment[None, :])
    logits = jnp.where(allowed, logits, -1e30)
    peak = jnp.max(logits, axis=-1, keepdims=True)
    weights = jnp.exp(logits - peak)
    probs = (weights / jnp.sum(weights, axis=-1, keepdims=True)).astype(jnp.bfloat16)
    value_heads = value_rows.reshape(length, KV_HEADS, HEAD_DIM)
    attended = jnp.einsum("gjqk,kgd->qgjd", probs, value_heads, preferred_element_type=jnp.float32)
    return (probs, attended.reshape(length, Q_HEADS * HEAD_DIM))


def values_grad(probs, d_out):
    length = d_out.shape[0]
    heads = d_out.reshape(length, KV_HEADS, GROUP, HEAD_DIM)
    summed = jnp.einsum("gjqk,qgjd->kgd", probs, heads, preferred_element_type=jnp.float32)
    return summed.reshape(length, VALUE_WIDTH).astype(jnp.bfloat16)


def add_pieces(rows_in, pieces):
    return (
        jnp.dot(rows_in, pieces[0], preferred_element_type=jnp.float32),
        jnp.dot(rows_in, pieces[1], preferred_element_type=jnp.float32),
    )


def body(
    train_input,
    train_query,
    train_keys,
    train_target,
    train_segments,
    value_weight,
    adapter_down,
    adapter_up,
    score_input,
    score_query,
    score_keys,
    score_segments,
):
    width = train_input.shape[-1]
    value_width = value_weight.shape[1]
    count_rows = train_segments.shape[0] * train_segments.shape[1]
    row_length = train_segments.shape[2]
    score_length = score_segments.shape[2]
    down_half = adapter_down.astype(jnp.bfloat16)
    upper_weight_half = adapter_up.astype(jnp.bfloat16)
    train_rows = train_input.reshape(-1, width)
    frozen_base_weight, low = add_pieces(
        train_rows,
        (
            lax.all_gather(value_weight, "fsdp", axis=0, tiled=True),
            lax.all_gather(down_half, "fsdp", axis=0, tiled=True),
        ),
    )
    lower_rank_half = low.astype(jnp.bfloat16)
    value_rows = (
        frozen_base_weight
        + adapter_scale_factor
        * jnp.dot(lower_rank_half, upper_weight_half, preferred_element_type=jnp.float32)
    ).astype(jnp.bfloat16)
    probs, attended = jax.vmap(attend_row)(
        train_query,
        train_keys,
        value_rows.reshape(count_rows, row_length, -1),
        train_segments.reshape(count_rows, row_length),
    )
    d_out = (attended - train_target.astype(jnp.float32)).astype(jnp.bfloat16)
    value_output_gradient = jax.vmap(values_grad)(probs, d_out).reshape(-1, value_width)
    low_rank_gradient = (
        adapter_scale_factor
        * lax.dot_general(
            value_output_gradient,
            upper_weight_half,
            (((1,), (1,)), ((), ())),
            preferred_element_type=jnp.float32,
        )
    ).astype(jnp.bfloat16)
    local_up_gradient = adapter_scale_factor * lax.dot_general(
        lower_rank_half,
        value_output_gradient,
        (((0,), (0,)), ((), ())),
        preferred_element_type=jnp.float32,
    )
    grad_down = lax.psum_scatter(
        lax.dot_general(
            train_rows,
            low_rank_gradient,
            (((0,), (0,)), ((), ())),
            preferred_element_type=jnp.float32,
        ),
        "fsdp",
        scatter_dimension=0,
        tiled=True,
    )
    grad_down = lax.psum(grad_down, "view")
    up_weight_gradient = lax.psum(local_up_gradient, ("fsdp", "view"))
    new_down = adapter_down - rate_down * grad_down
    new_up = adapter_up - rate_up * up_weight_gradient
    new_down_half = new_down.astype(jnp.bfloat16)
    new_up_half = new_up.astype(jnp.bfloat16)
    score_rows = score_input.reshape(-1, width)
    score_base, score_low = add_pieces(
        score_rows,
        (
            lax.all_gather(value_weight, "fsdp", axis=0, tiled=True),
            lax.all_gather(new_down_half, "fsdp", axis=0, tiled=True),
        ),
    )
    score_values = (
        score_base
        + adapter_scale_factor
        * jnp.dot(score_low.astype(jnp.bfloat16), new_up_half, preferred_element_type=jnp.float32)
    ).astype(jnp.bfloat16)
    score_probs, score_attended = jax.vmap(attend_row)(
        score_query,
        score_keys,
        score_values.reshape(count_rows, score_length, -1),
        score_segments.reshape(count_rows, score_length),
    )
    scored = score_attended.astype(jnp.bfloat16)
    return (new_down, new_up, scored)


F32, BF16 = jnp.float32, jnp.bfloat16
N, DEPTH = 8, 4
BLOCK = 64
WINDOW = 2 * BLOCK
NT = (((1,), (1,)), ((), ()))
TN = (((0,), (0,)), ((), ()))
UP, DOWN, SIDE, TWIN, CORE = range(5)


def nt_dot(a, b):
    return lax.dot_general(a, b, NT, preferred_element_type=F32)


def tn_dot(a, b):
    return lax.dot_general(a, b, TN, preferred_element_type=F32)


def dot(a, b):
    return jnp.dot(a, b, preferred_element_type=F32)


def lanes(start, size):
    return pl.ds(pl.multiple_of(start, size), size)


def stack_heads(ref, rows, g):
    return jnp.concatenate(
        [ref[rows, lanes((g * GROUP + j) * HEAD_DIM, HEAD_DIM)] for j in range(GROUP)], axis=0
    )


def softmax_rows(logits, allowed):
    shape = logits.shape
    logits = (logits * HEAD_DIM ** (-0.5)).reshape(GROUP, BLOCK, shape[-1])
    logits = jnp.where(allowed[None], logits, -1e30)
    weights = jnp.exp(logits - jnp.max(logits, axis=-1, keepdims=True))
    probs = weights * (1.0 / jnp.sum(weights, axis=-1, keepdims=True))
    return probs.reshape(shape).astype(BF16)


def fused_kernel(
    x_hbm, q_hbm, k_hbm, goal_hbm, seg_hbm, w_hbm, down_hbm, up_hbm, sx_hbm, sq_hbm, sk_hbm, sseg_hbm,
    new_down_t, new_up, scored,
    xs, qs, ks, goal, seg, down_t, up_ref, sq, sk, sseg, seg_col, wbuf, dbuf, ndbuf, probs, sprobs, base, vals, dvals,
    low_s, slow_s, gmine, gsend, gpair, rsend, rrecv, fhalf, frecv, gu, gupair, gusum, gurecv, gupart, guall,
    s_loc, s_w, r_w, s_d, r_d, s_nd, r_nd, s_gp, r_gp, s_rs, r_rs, s_f, r_f,
    s_up, r_up, s_ur, r_ur, s_ua, r_ua, s_uc, r_uc,
):
    t, f, c = lax.axis_index("task"), lax.axis_index("fsdp"), lax.axis_index("view")
    z, x = lax.div(f, 2), lax.rem(f, 2)
    other_t, other_x, other_c = 1 - t, 1 - x, 1 - c
    width = xs.shape[1]
    part = width // N
    half = part // 2
    rows = vals.shape[0]
    late = []
    wcols = VALUE_WIDTH // 2

    def device(kind):
        return {
            UP: {"fsdp": f + 2},
            DOWN: {"fsdp": f - 2},
            SIDE: {"fsdp": 2 * z + other_x},
            TWIN: {"task": other_t},
            CORE: {"view": other_c},
        }[kind]

    def exists(kind):
        return {UP: z < DEPTH - 1, DOWN: z > 0}.get(kind, True)

    def start(make, pred=True):
        if pred is True:
            make().start()
        else:
            pl.when(pred)(lambda: make().start())
        late.append((make, pred))

    def send(kind, src, dst, s_sem, r_sem, pred=True):
        where = exists(kind)
        if where is not True:
            pred = where if pred is True else jnp.logical_and(where, pred)

        def make():
            return pltpu.make_async_remote_copy(
                src_ref=src, dst_ref=dst, send_sem=s_sem, recv_sem=r_sem,
                device_id=device(kind), device_id_type=pl.DeviceIdType.MESH,
            )

        start(make, pred)

    def peer_send(peer, src, dst, s_sem, r_sem):
        def make():
            return pltpu.make_async_remote_copy(
                src_ref=src, dst_ref=dst, send_sem=s_sem, recv_sem=r_sem,
                device_id={"fsdp": peer}, device_id_type=pl.DeviceIdType.MESH,
            )

        start(make)

    def arrived(dst, r_sem, pred=True):
        def wait():
            pltpu.make_async_remote_copy(
                src_ref=dst, dst_ref=dst, send_sem=r_sem, recv_sem=r_sem,
                device_id={"view": other_c}, device_id_type=pl.DeviceIdType.MESH,
            ).wait_recv()

        if pred is True:
            wait()
        else:
            pl.when(pred)(wait)

    def peers():
        return [lax.rem(f + k, N) for k in range(1, N)]

    barrier = pltpu.get_barrier_semaphore()
    for peer in peers():
        pl.semaphore_signal(barrier, inc=1, device_id={"fsdp": peer}, device_id_type=pl.DeviceIdType.MESH)
    for kind in (TWIN, CORE):
        pl.semaphore_signal(barrier, inc=1, device_id=device(kind), device_id_type=pl.DeviceIdType.MESH)

    local = [
        (down_hbm, down_t),
        (q_hbm, qs),
        (k_hbm, ks),
        (seg_hbm, seg),
        (sq_hbm, sq),
        (sk_hbm, sk),
        (sseg_hbm, sseg),
        (x_hbm, xs.at[pl.ds(0, rows)]),
        (sx_hbm, xs.at[pl.ds(rows, BLOCK)]),
        (up_hbm, up_ref),
        (goal_hbm, goal),
    ] + [(w_hbm.at[:, :, pl.ds(h * wcols, wcols)], wbuf.at[h, pl.ds(4 * f, 4)]) for h in range(2)]
    loads = [pltpu.make_async_copy(a, b, s_loc.at[i]) for i, (a, b) in enumerate(local)]
    for load in loads:
        load.start()
    loads[0].wait()
    for side in range(2):
        dbuf[2 * f + side] = down_t[:, side * half:(side + 1) * half].astype(BF16)
    pl.semaphore_wait(barrier, N + 1)

    line = [(d, s, z - s * d) for d in range(1, DEPTH) for s in (1, -1)]

    def inside(zp):
        return jnp.logical_and(zp >= 0, zp < DEPTH)

    def piece_send(buf, s_sem, r_sem, kind, i, pred=True):
        send(kind, buf.at[i], buf.at[i], s_sem.at[kind, i], r_sem.at[i], pred)

    def pieces_own(buf, s_sem, r_sem):
        for kind in (UP, DOWN, SIDE):
            piece_send(buf, s_sem, r_sem, kind, 2 * f + c)

    def pieces_line(buf, s_sem, r_sem, d):
        for dd, s, zp in line:
            if dd == d:
                ok, i = inside(zp), 2 * (2 * zp + x) + c
                arrived(buf.at[i], r_sem.at[i], ok)
                for kind in (UP if s > 0 else DOWN, SIDE, CORE):
                    piece_send(buf, s_sem, r_sem, kind, i, ok)

    def pieces_side(buf, s_sem, r_sem, d):
        for dd, s, zp in [(0, 1, z)] + line:
            if dd == d:
                ok, i = (True if d == 0 else inside(zp)), 2 * (2 * zp + other_x) + c
                arrived(buf.at[i], r_sem.at[i], ok)
                piece_send(buf, s_sem, r_sem, CORE, i, ok)

    def pieces_core(buf, r_sem):
        for peer in peers():
            i = 2 * peer + other_c
            arrived(buf.at[i], r_sem.at[i])

    mine, theirs = 2 * t + c, 2 * other_t + c

    def w_send(h, kind, i, pred=True):
        send(kind, wbuf.at[h, i], wbuf.at[h, i], s_w.at[h, kind, i], r_w.at[h, i], pred)

    def w_wait(h, i, pred=True):
        arrived(wbuf.at[h, i], r_w.at[h, i], pred)

    def w_own(h):
        for kind, q in ((UP, mine), (DOWN, mine), (SIDE, mine), (SIDE, theirs)):
            i = 4 * f + q
            src = w_hbm.at[q, :, pl.ds(h * wcols, wcols)]
            send(kind, src, wbuf.at[h, i], s_w.at[h, kind, i], r_w.at[h, i])

    def w_line(h, d):
        for dd, s, zp in line:
            if dd == d:
                ok, i = inside(zp), 4 * (2 * zp + x) + mine
                w_wait(h, i, ok)
                for kind in (UP if s > 0 else DOWN, SIDE, TWIN, CORE):
                    w_send(h, kind, i, ok)

    def w_side(h, d):
        if d == 0:
            i = 4 * (2 * z + other_x) + mine
            w_wait(h, i)
            w_send(h, CORE, i)
            i = 4 * (2 * z + other_x) + theirs
            w_wait(h, i)
            for kind in (UP, DOWN, CORE):
                w_send(h, kind, i)
            return
        for dd, s, zp in line:
            if dd == d:
                ok, i = inside(zp), 4 * (2 * zp + other_x) + mine
                w_wait(h, i, ok)
                if d > 1:
                    w_send(h, TWIN, i, ok)
                w_send(h, CORE, i, ok)

    def w_twin(h, d, xx):
        for dd, s, zp in line:
            if dd == d:
                ok, i = inside(zp), 4 * (2 * zp + xx) + theirs
                w_wait(h, i, ok)
                w_send(h, CORE, i, ok)

    def shards(d):
        if d == 0:
            return [(True, f), (True, 2 * z + other_x)]
        return [(inside(zp), 2 * zp + xx) for dd, s, zp in line if dd == d for xx in (x, other_x)]

    def run(pred, step):
        if pred is True:
            step()
        else:
            pl.when(pred)(step)

    def add_base(h, d):
        for n, (ok, shard) in enumerate(shards(d)):
            def step(n=n, shard=shard):
                if d or n:
                    for q in (2 * t + other_c, 2 * other_t + other_c):
                        w_wait(h, 4 * shard + q)
                weight = wbuf[h, pl.ds(4 * shard, 4)].reshape(part, wcols)
                base[:, h * wcols:(h + 1) * wcols] += dot(xs[:, lanes(shard * part, part)], weight)

            run(ok, step)

    def train_probs(b):
        first = max(b - 1, 0) * BLOCK
        position_q = b * BLOCK + lax.broadcasted_iota(jnp.int32, (BLOCK, WINDOW), 0)
        position_k = first + lax.broadcasted_iota(jnp.int32, (BLOCK, WINDOW), 1)
        same = seg_col[pl.ds(b * BLOCK, BLOCK), :] == seg[...].astype(F32)[:, first:first + WINDOW]
        allowed = (position_k <= position_q) & same

        def head_group(g, _):
            q = stack_heads(qs, pl.ds(b * BLOCK, BLOCK), g)
            k = ks[pl.ds(first, WINDOW), lanes(g * HEAD_DIM, HEAD_DIM)]
            probs[b * KV_HEADS + g] = softmax_rows(nt_dot(q, k), allowed)
            return 0

        lax.fori_loop(0, KV_HEADS, head_group, 0)

    def score_probs():
        order_q = lax.broadcasted_iota(jnp.int32, (BLOCK, BLOCK), 0)
        order_k = lax.broadcasted_iota(jnp.int32, (BLOCK, BLOCK), 1)
        ids = sseg[...].astype(F32)
        column = jnp.broadcast_to(jnp.concatenate([ids, ids], axis=1), (WINDOW, WINDOW)).T
        allowed = (order_k <= order_q) & (column[:BLOCK, :BLOCK] == ids)

        def head_group(g, _):
            q = stack_heads(sq, pl.ds(0, BLOCK), g)
            sprobs[g] = softmax_rows(nt_dot(q, sk[:, lanes(g * HEAD_DIM, HEAD_DIM)]), allowed)
            return 0

        lax.fori_loop(0, KV_HEADS, head_group, 0)

    def low_step(i, acc):
        return acc + nt_dot(xs[pl.ds(0, rows), lanes(i * half, half)], dbuf[i])

    def attention(h):
        halves = pl.ds(h * wcols, wcols)
        up_half = up_ref[:, halves].astype(BF16)
        mixed = adapter_scale_factor * dot(low_s[...], up_half)
        vals[:, halves] = (base[pl.ds(0, rows), halves] + mixed).astype(BF16)
        for b in range(rows // BLOCK):
            first = max(b - 1, 0) * BLOCK

            def head_group(g, _, b=b, first=first):
                p = probs[b * KV_HEADS + g]
                cols = lanes(g * HEAD_DIM, HEAD_DIM)
                attended = dot(p, vals[pl.ds(first, WINDOW), cols])
                d_out = (attended - stack_heads(goal, pl.ds(b * BLOCK, BLOCK), g).astype(F32)).astype(BF16)
                dvals[pl.ds(first, WINDOW), cols] += tn_dot(p, d_out)
                return 0

            lax.fori_loop(h * KV_HEADS // 2, (h + 1) * KV_HEADS // 2, head_group, 0)

    dset = (dbuf, s_d, r_d)
    pieces_own(*dset)
    w_own(0)
    base[...] = jnp.zeros_like(base)
    dvals[...] = jnp.zeros_like(dvals)
    for i in range(1, 4):
        loads[i].wait()
    seg_col[...] = jnp.broadcast_to(seg[...].astype(F32), (WINDOW, rows)).T
    train_probs(0)
    pieces_line(*dset, 1)
    w_line(0, 1)
    pieces_side(*dset, 0)
    w_side(0, 0)
    w_own(1)
    train_probs(1)
    pieces_line(*dset, 2)
    w_line(0, 2)
    pieces_side(*dset, 1)
    w_side(0, 1)
    w_twin(0, 1, x)
    w_twin(0, 1, other_x)
    train_probs(2)
    pieces_line(*dset, 3)
    w_line(0, 3)
    pieces_side(*dset, 2)
    w_side(0, 2)
    w_twin(0, 2, x)
    w_line(1, 1)
    w_side(1, 0)
    train_probs(3)
    pieces_side(*dset, 3)
    w_side(0, 3)
    w_twin(0, 2, other_x)
    w_twin(0, 3, x)
    w_line(1, 2)
    w_side(1, 1)
    for i in range(4, len(loads)):
        loads[i].wait()
    score_probs()
    w_twin(1, 1, x)
    w_twin(1, 1, other_x)
    w_line(1, 3)
    w_twin(0, 3, other_x)
    pieces_core(dbuf, r_d)
    low = lax.fori_loop(0, 2 * N, low_step, jnp.zeros((rows, low_s.shape[1]), F32)).astype(BF16)
    low_s[...] = low
    w_side(1, 2)
    w_twin(1, 2, x)
    for d in range(DEPTH):
        add_base(0, d)
    w_side(1, 3)
    w_twin(1, 2, other_x)
    w_twin(1, 3, x)
    attention(0)
    w_twin(1, 3, other_x)
    for d in range(DEPTH):
        add_base(1, d)
    attention(1)
    up_half = up_ref[...].astype(BF16)
    dv = dvals[...].astype(BF16)
    dlow_t = (adapter_scale_factor * nt_dot(up_half, dv)).astype(BF16)

    def grad_of(peer, side):
        return dot(dlow_t, xs[pl.ds(0, rows), lanes(peer * part + side * half, half)])

    order = peers() + [f]
    for n, peer in enumerate(order):
        gsend[n] = grad_of(peer, other_c).astype(BF16)
        send(CORE, gsend.at[n], gpair.at[n], s_gp.at[n], r_gp.at[n])
    gu[...] = adapter_scale_factor * tn_dot(low_s[...], dv)
    ucols = VALUE_WIDTH // 2
    send(CORE, gu.at[:, lanes(other_c * ucols, ucols)], gupair, s_up, r_up)
    for n, peer in enumerate(order[:-1]):
        gmine[n] = grad_of(peer, c)
        arrived(gpair.at[n], r_gp.at[n])
        rsend[n] = (gmine[n] + gpair[n].astype(F32)).astype(BF16)
        peer_send(peer, rsend.at[n], rrecv.at[n], s_rs.at[n], r_rs.at[n])
    arrived(gupair, r_up)
    gusum[...] = gu[:, lanes(c * ucols, ucols)] + gupair[...]
    urows = gusum.shape[0] // N
    for n, peer in enumerate(order[:-1]):
        peer_send(
            peer, gusum.at[pl.ds(pl.multiple_of(peer * urows, urows), urows)], gurecv.at[n], s_ur.at[n], r_ur.at[n]
        )
    gmine[N - 1] = grad_of(f, c)
    arrived(gpair.at[N - 1], r_gp.at[N - 1])
    total = gmine[N - 1] + gpair[N - 1].astype(F32)
    for n in range(N - 1):
        arrived(rrecv.at[n], r_rs.at[n])
        total = total + rrecv[n].astype(F32)
    new_half = down_t[:, lanes(c * half, half)] - rate_down * total
    fhalf[...] = new_half
    ndbuf[2 * f + c] = new_half.astype(BF16)
    ndset = (ndbuf, s_nd, r_nd)
    pieces_own(*ndset)
    send(CORE, fhalf, frecv, s_f, r_f)

    utotal = gusum[pl.ds(pl.multiple_of(f * urows, urows), urows), :]
    for n in range(N - 1):
        arrived(gurecv.at[n], r_ur.at[n])
        utotal = utotal + gurecv[n]
    gupart[...] = utotal
    guall[c, pl.ds(pl.multiple_of(f * urows, urows), urows), :] = utotal
    for n, peer in enumerate(order[:-1]):
        peer_send(
            peer, gupart, guall.at[c, pl.ds(pl.multiple_of(f * urows, urows), urows)], s_ua.at[n], r_ua.at[f]
        )
    slow_s[...] = jnp.zeros_like(slow_s)

    def add_slow(d):
        for n, (ok, shard) in enumerate(shards(d)):
            def step(n=n, shard=shard):
                if d or n:
                    i = 2 * shard + other_c
                    arrived(ndbuf.at[i], r_nd.at[i])
                acc = slow_s[...]
                for side in range(2):
                    cols = lanes(shard * part + side * half, half)
                    acc = acc + nt_dot(xs[pl.ds(rows, BLOCK), cols], ndbuf[2 * shard + side])
                slow_s[...] = acc

            run(ok, step)

    pieces_line(*ndset, 1)
    pieces_side(*ndset, 0)
    pieces_line(*ndset, 2)
    pieces_side(*ndset, 1)
    arrived(frecv, r_f)
    new_down_t[:, lanes(c * half, half)] = fhalf[...]
    new_down_t[:, lanes(other_c * half, half)] = frecv[...]
    ndbuf[2 * f + other_c] = frecv[...].astype(BF16)
    add_slow(0)
    pieces_line(*ndset, 3)
    pieces_side(*ndset, 2)
    for peer in peers():
        arrived(guall.at[c, pl.ds(pl.multiple_of(peer * urows, urows), urows)], r_ua.at[peer])
    send(CORE, guall.at[c], guall.at[c], s_uc, r_uc)
    add_slow(1)
    pieces_side(*ndset, 3)
    arrived(guall.at[other_c], r_uc)
    for side in range(2):
        cols = pl.ds(side * ucols, ucols)
        new_up[:, cols] = up_ref[:, cols] - rate_up * guall[side]
    add_slow(2)
    add_slow(3)
    slow = slow_s[...].astype(BF16)
    svals = (
        base[pl.ds(rows, BLOCK), :] + adapter_scale_factor * dot(slow, new_up[...].astype(BF16))
    ).astype(BF16)
    for g in range(KV_HEADS):
        attended = dot(sprobs[g], svals[:, g * HEAD_DIM:(g + 1) * HEAD_DIM]).astype(BF16)
        for j in range(GROUP):
            at = (g * GROUP + j) * HEAD_DIM
            scored[:, at:at + HEAD_DIM] = attended[j * BLOCK:(j + 1) * BLOCK]

    def finish(make):
        make().wait_send()

    for make, pred in late:
        if pred is True:
            finish(make)
        else:
            pl.when(pred)(lambda make=make: finish(make))


def fused_body(
    train_input, train_query, train_keys, train_target, train_segments, value_weight, adapter_down, adapter_up,
    score_input, score_query, score_keys, score_segments,
):
    rows, width = train_input.shape[1:]
    part, rank = adapter_down.shape
    half = part // 2
    heads = train_query.shape[2]
    srows = score_input.shape[1]
    vw = value_weight.shape[1]
    hbm, vmem = pl.BlockSpec(memory_space=pl.ANY), pl.BlockSpec(memory_space=pltpu.VMEM)
    sem = pltpu.SemaphoreType.DMA
    uc, ur = vw // 2, rank // N
    scratch = [
        pltpu.VMEM((rows + srows, width), BF16),
        pltpu.VMEM((rows, heads), BF16),
        pltpu.VMEM((rows, vw), BF16),
        pltpu.VMEM((rows, heads), BF16),
        pltpu.VMEM((1, rows), jnp.int32),
        pltpu.VMEM((rank, part), F32),
        pltpu.VMEM((rank, vw), F32),
        pltpu.VMEM((srows, heads), BF16),
        pltpu.VMEM((srows, vw), BF16),
        pltpu.VMEM((1, srows), jnp.int32),
        pltpu.VMEM((rows, WINDOW), F32),
        pltpu.VMEM((2, 4 * N, part // 4, vw // 2), BF16),
        pltpu.VMEM((2 * N, rank, half), BF16),
        pltpu.VMEM((2 * N, rank, half), BF16),
        pltpu.VMEM((rows // BLOCK * KV_HEADS, GROUP * BLOCK, WINDOW), BF16),
        pltpu.VMEM((KV_HEADS, GROUP * BLOCK, BLOCK), BF16),
        pltpu.VMEM((rows + srows, vw), F32),
        pltpu.VMEM((rows, vw), BF16),
        pltpu.VMEM((rows, vw), F32),
        pltpu.VMEM((rows, rank), BF16),
        pltpu.VMEM((srows, rank), F32),
        pltpu.VMEM((N, rank, half), F32),
        pltpu.VMEM((N, rank, half), BF16),
        pltpu.VMEM((N, rank, half), BF16),
        pltpu.VMEM((N - 1, rank, half), BF16),
        pltpu.VMEM((N - 1, rank, half), BF16),
        pltpu.VMEM((rank, half), F32),
        pltpu.VMEM((rank, half), F32),
        pltpu.VMEM((rank, vw), F32),
        pltpu.VMEM((rank, uc), F32),
        pltpu.VMEM((rank, uc), F32),
        pltpu.VMEM((N - 1, ur, uc), F32),
        pltpu.VMEM((ur, uc), F32),
        pltpu.VMEM((2, rank, uc), F32),
        sem((13,)),
        sem((2, 5, 4 * N)), sem((2, 4 * N)),
        sem((5, 2 * N)), sem((2 * N,)),
        sem((5, 2 * N)), sem((2 * N,)),
        sem((N,)), sem((N,)),
        sem((N - 1,)), sem((N - 1,)),
        sem, sem,
        sem, sem,
        sem((N - 1,)), sem((N - 1,)),
        sem((N - 1,)), sem((N,)),
        sem, sem,
    ]
    new_down_t, new_up, scored = pl.pallas_call(
        fused_kernel,
        out_shape=(
            jax.ShapeDtypeStruct((rank, part), F32),
            jax.ShapeDtypeStruct(adapter_up.shape, F32),
            jax.ShapeDtypeStruct((srows, heads), BF16),
        ),
        in_specs=[hbm] * 12,
        out_specs=(vmem, vmem, vmem),
        scratch_shapes=scratch,
        compiler_params=pltpu.CompilerParams(
            collective_id=0, has_side_effects=True, vmem_limit_bytes=63 * 1024 * 1024
        ),
        name="test_time_step",
    )(
        train_input[0], train_query[0], train_keys[0], train_target[0], train_segments.reshape(1, rows),
        value_weight.reshape(4, part // 4, vw), adapter_down.T, adapter_up,
        score_input[0], score_query[0], score_keys[0], score_segments.reshape(1, srows),
    )
    return (new_down_t.T, new_up, scored[None])


def solution(mesh):
    in_specs = (
        P(("task", "view"), "fsdp", None),
        P(("task", "view"), "fsdp", None),
        P(("task", "view"), "fsdp", None),
        P(("task", "view"), "fsdp", None),
        P(("task", "view"), "fsdp", None),
        P("fsdp", None),
        P(("task", "fsdp"), None),
        P("task", None),
        P(("task", "view"), "fsdp", None),
        P(("task", "view"), "fsdp", None),
        P(("task", "view"), "fsdp", None),
        P(("task", "view"), "fsdp", None),
    )
    out_specs = (P(("task", "fsdp"), None), P("task", None), P(("task", "view"), "fsdp", None))
    local = fused_body if (mesh.shape["fsdp"], mesh.shape["view"]) == (8, 2) else body
    return jax.shard_map(local, mesh=mesh, in_specs=in_specs, out_specs=out_specs, check_vma=False)
```

```python
import jax
import jax.numpy as jnp
from jax import lax
from jax.experimental import pallas as pl
from jax.experimental.pallas import tpu as pltpu
from jax.sharding import PartitionSpec as P

Q_HEADS = 32
KV_HEADS = 4
HEAD_DIM = 128
GROUP = 8
VALUE_WIDTH = 512


adapter_scale_factor = 0.5
rate_down = 2e-05
rate_up = 0.001


def attend_row(query, keyset, value_rows, segment):
    length = query.shape[0]
    query_heads = query.reshape(length, KV_HEADS, GROUP, HEAD_DIM)
    key_heads = keyset.reshape(length, KV_HEADS, HEAD_DIM)
    logits = jnp.einsum(
        "qgjd,kgd->gjqk", query_heads, key_heads, preferred_element_type=jnp.float32
    ) * HEAD_DIM ** (-0.5)
    positions = jnp.arange(length, dtype=jnp.int32)
    allowed = (positions[None, :] <= positions[:, None]) & (segment[:, None] == segment[None, :])
    logits = jnp.where(allowed, logits, -1e30)
    peak = jnp.max(logits, axis=-1, keepdims=True)
    weights = jnp.exp(logits - peak)
    probs = (weights / jnp.sum(weights, axis=-1, keepdims=True)).astype(jnp.bfloat16)
    value_heads = value_rows.reshape(length, KV_HEADS, HEAD_DIM)
    attended = jnp.einsum("gjqk,kgd->qgjd", probs, value_heads, preferred_element_type=jnp.float32)
    return (probs, attended.reshape(length, Q_HEADS * HEAD_DIM))


def values_grad(probs, d_out):
    length = d_out.shape[0]
    heads = d_out.reshape(length, KV_HEADS, GROUP, HEAD_DIM)
    summed = jnp.einsum("gjqk,qgjd->kgd", probs, heads, preferred_element_type=jnp.float32)
    return summed.reshape(length, VALUE_WIDTH).astype(jnp.bfloat16)


def add_pieces(rows_in, pieces):
    return (
        jnp.dot(rows_in, pieces[0], preferred_element_type=jnp.float32),
        jnp.dot(rows_in, pieces[1], preferred_element_type=jnp.float32),
    )


def body(
    train_input,
    train_query,
    train_keys,
    train_target,
    train_segments,
    value_weight,
    adapter_down,
    adapter_up,
    score_input,
    score_query,
    score_keys,
    score_segments,
):
    width = train_input.shape[-1]
    value_width = value_weight.shape[1]
    count_rows = train_segments.shape[0] * train_segments.shape[1]
    row_length = train_segments.shape[2]
    score_length = score_segments.shape[2]
    down_half = adapter_down.astype(jnp.bfloat16)
    upper_weight_half = adapter_up.astype(jnp.bfloat16)
    train_rows = train_input.reshape(-1, width)
    frozen_base_weight, low = add_pieces(
        train_rows,
        (
            lax.all_gather(value_weight, "fsdp", axis=0, tiled=True),
            lax.all_gather(down_half, "fsdp", axis=0, tiled=True),
        ),
    )
    lower_rank_half = low.astype(jnp.bfloat16)
    value_rows = (
        frozen_base_weight
        + adapter_scale_factor
        * jnp.dot(lower_rank_half, upper_weight_half, preferred_element_type=jnp.float32)
    ).astype(jnp.bfloat16)
    probs, attended = jax.vmap(attend_row)(
        train_query,
        train_keys,
        value_rows.reshape(count_rows, row_length, -1),
        train_segments.reshape(count_rows, row_length),
    )
    d_out = (attended - train_target.astype(jnp.float32)).astype(jnp.bfloat16)
    value_output_gradient = jax.vmap(values_grad)(probs, d_out).reshape(-1, value_width)
    low_rank_gradient = (
        adapter_scale_factor
        * lax.dot_general(
            value_output_gradient,
            upper_weight_half,
            (((1,), (1,)), ((), ())),
            preferred_element_type=jnp.float32,
        )
    ).astype(jnp.bfloat16)
    local_up_gradient = adapter_scale_factor * lax.dot_general(
        lower_rank_half,
        value_output_gradient,
        (((0,), (0,)), ((), ())),
        preferred_element_type=jnp.float32,
    )
    grad_down = lax.psum_scatter(
        lax.dot_general(
            train_rows,
            low_rank_gradient,
            (((0,), (0,)), ((), ())),
            preferred_element_type=jnp.float32,
        ),
        "fsdp",
        scatter_dimension=0,
        tiled=True,
    )
    grad_down = lax.psum(grad_down, "view")
    up_weight_gradient = lax.psum(local_up_gradient, ("fsdp", "view"))
    new_down = adapter_down - rate_down * grad_down
    new_up = adapter_up - rate_up * up_weight_gradient
    new_down_half = new_down.astype(jnp.bfloat16)
    new_up_half = new_up.astype(jnp.bfloat16)
    score_rows = score_input.reshape(-1, width)
    score_base, score_low = add_pieces(
        score_rows,
        (
            lax.all_gather(value_weight, "fsdp", axis=0, tiled=True),
            lax.all_gather(new_down_half, "fsdp", axis=0, tiled=True),
        ),
    )
    score_values = (
        score_base
        + adapter_scale_factor
        * jnp.dot(score_low.astype(jnp.bfloat16), new_up_half, preferred_element_type=jnp.float32)
    ).astype(jnp.bfloat16)
    score_probs, score_attended = jax.vmap(attend_row)(
        score_query,
        score_keys,
        score_values.reshape(count_rows, score_length, -1),
        score_segments.reshape(count_rows, score_length),
    )
    scored = score_attended.astype(jnp.bfloat16)
    return (new_down, new_up, scored)


F32, BF16 = jnp.float32, jnp.bfloat16
N, DEPTH = 8, 4
BLOCK = 64
WINDOW = 2 * BLOCK
NT = (((1,), (1,)), ((), ()))
TN = (((0,), (0,)), ((), ()))
UP, DOWN, SIDE, TWIN, CORE = range(5)


def nt_dot(a, b):
    return lax.dot_general(a, b, NT, preferred_element_type=F32)


def tn_dot(a, b):
    return lax.dot_general(a, b, TN, preferred_element_type=F32)


def dot(a, b):
    return jnp.dot(a, b, preferred_element_type=F32)


def lanes(start, size):
    return pl.ds(pl.multiple_of(start, size), size)


def stack_heads(ref, rows, g):
    return jnp.concatenate(
        [ref[rows, lanes((g * GROUP + j) * HEAD_DIM, HEAD_DIM)] for j in range(GROUP)], axis=0
    )


def softmax_rows(logits, allowed):
    shape = logits.shape
    logits = (logits * HEAD_DIM ** (-0.5)).reshape(GROUP, BLOCK, shape[-1])
    logits = jnp.where(allowed[None], logits, -1e30)
    weights = jnp.exp(logits - jnp.max(logits, axis=-1, keepdims=True))
    probs = weights * (1.0 / jnp.sum(weights, axis=-1, keepdims=True))
    return probs.reshape(shape).astype(BF16)


def fused_kernel(
    x_hbm, q_hbm, k_hbm, goal_hbm, seg_hbm, w_hbm, down_hbm, up_hbm, sx_hbm, sq_hbm, sk_hbm, sseg_hbm,
    new_down_t, new_up, scored,
    xs, qs, ks, goal, seg, down_t, up_ref, sq, sk, sseg, seg_col, wbuf, dbuf, ndbuf, probs, sprobs, base, vals, dvals,
    low_s, slow_s, slow_recv, gsend, gpair, rsend, rside, rline, rrecv, fhalf, frecv,
    gu, gupair, gusum, guside, guline, guall,
    s_loc, s_w, r_w, s_wc, r_wc, s_d, r_d, s_nd, r_nd, s_gp, r_gp, s_rx, r_rx, s_rs, r_rs, s_f, r_f,
    s_up, r_up, s_ur, r_ur, s_ua, r_ua, s_uc, r_uc, s_sx, r_sx, s_sl, r_sl,
):
    t, f, c = lax.axis_index("task"), lax.axis_index("fsdp"), lax.axis_index("view")
    z, x = lax.div(f, 2), lax.rem(f, 2)
    other_t, other_x, other_c = 1 - t, 1 - x, 1 - c
    width = xs.shape[1]
    part = width // N
    half = part // 2
    rows = vals.shape[0]
    late = []
    wcols = VALUE_WIDTH // 2

    def device(kind):
        return {
            UP: {"fsdp": f + 2},
            DOWN: {"fsdp": f - 2},
            SIDE: {"fsdp": 2 * z + other_x},
            TWIN: {"task": other_t},
            CORE: {"view": other_c},
        }[kind]

    def exists(kind):
        return {UP: z < DEPTH - 1, DOWN: z > 0}.get(kind, True)

    def start(make, pred=True):
        if pred is True:
            make().start()
        else:
            pl.when(pred)(lambda: make().start())
        late.append((make, pred))

    def send(kind, src, dst, s_sem, r_sem, pred=True):
        where = exists(kind)
        if where is not True:
            pred = where if pred is True else jnp.logical_and(where, pred)

        def make():
            return pltpu.make_async_remote_copy(
                src_ref=src, dst_ref=dst, send_sem=s_sem, recv_sem=r_sem,
                device_id=device(kind), device_id_type=pl.DeviceIdType.MESH,
            )

        start(make, pred)

    def peer_send(peer, src, dst, s_sem, r_sem):
        def make():
            return pltpu.make_async_remote_copy(
                src_ref=src, dst_ref=dst, send_sem=s_sem, recv_sem=r_sem,
                device_id={"fsdp": peer}, device_id_type=pl.DeviceIdType.MESH,
            )

        start(make)

    def arrived(dst, r_sem, pred=True):
        def wait():
            pltpu.make_async_remote_copy(
                src_ref=dst, dst_ref=dst, send_sem=r_sem, recv_sem=r_sem,
                device_id={"view": other_c}, device_id_type=pl.DeviceIdType.MESH,
            ).wait_recv()

        if pred is True:
            wait()
        else:
            pl.when(pred)(wait)

    def flush():
        def finish(make):
            make().wait_send()

        for make, pred in late:
            if pred is True:
                finish(make)
            else:
                pl.when(pred)(lambda make=make: finish(make))
        late.clear()

    def peers():
        return [lax.rem(f + k, N) for k in range(1, N)]

    barrier = pltpu.get_barrier_semaphore()
    for peer in peers():
        pl.semaphore_signal(barrier, inc=1, device_id={"fsdp": peer}, device_id_type=pl.DeviceIdType.MESH)
    for kind in (TWIN, CORE):
        pl.semaphore_signal(barrier, inc=1, device_id=device(kind), device_id_type=pl.DeviceIdType.MESH)

    local = [
        (down_hbm, down_t),
        (q_hbm, qs),
        (k_hbm, ks),
        (seg_hbm, seg),
        (sq_hbm, sq),
        (sk_hbm, sk),
        (sseg_hbm, sseg),
        (x_hbm, xs.at[pl.ds(0, rows)]),
        (sx_hbm, xs.at[pl.ds(rows, BLOCK)]),
        (up_hbm, up_ref),
        (goal_hbm, goal),
    ] + [(w_hbm.at[:, :, pl.ds(h * wcols, wcols)], wbuf.at[h, pl.ds(4 * f, 4)]) for h in range(2)]
    loads = [pltpu.make_async_copy(a, b, s_loc.at[i]) for i, (a, b) in enumerate(local)]
    for load in loads:
        load.start()
    loads[0].wait()
    for side in range(2):
        dbuf[2 * f + side] = down_t[:, side * half:(side + 1) * half].astype(BF16)
    pl.semaphore_wait(barrier, N + 1)

    line = [(d, s, z - s * d) for d in range(1, DEPTH) for s in (1, -1)]

    def inside(zp):
        return jnp.logical_and(zp >= 0, zp < DEPTH)

    def piece_send(buf, s_sem, r_sem, kind, i, pred=True):
        send(kind, buf.at[i], buf.at[i], s_sem.at[kind, i], r_sem.at[i], pred)

    def pieces_own(buf, s_sem, r_sem):
        for kind in (UP, DOWN, SIDE):
            piece_send(buf, s_sem, r_sem, kind, 2 * f + c)

    def pieces_line(buf, s_sem, r_sem, d):
        for dd, s, zp in line:
            if dd == d:
                ok, i = inside(zp), 2 * (2 * zp + x) + c
                arrived(buf.at[i], r_sem.at[i], ok)
                for kind in (UP if s > 0 else DOWN, SIDE, CORE):
                    piece_send(buf, s_sem, r_sem, kind, i, ok)

    def pieces_side(buf, s_sem, r_sem, d):
        for dd, s, zp in [(0, 1, z)] + line:
            if dd == d:
                ok, i = (True if d == 0 else inside(zp)), 2 * (2 * zp + other_x) + c
                arrived(buf.at[i], r_sem.at[i], ok)
                piece_send(buf, s_sem, r_sem, CORE, i, ok)

    def pieces_core(buf, r_sem):
        for peer in peers():
            i = 2 * peer + other_c
            arrived(buf.at[i], r_sem.at[i])

    mine, theirs = 2 * c + t, 2 * c + other_t

    def w_send(h, kind, i, pred=True):
        send(kind, wbuf.at[h, i], wbuf.at[h, i], s_w.at[h, kind, i], r_w.at[h, i], pred)

    def w_wait(h, i, pred=True):
        arrived(wbuf.at[h, i], r_w.at[h, i], pred)

    def w_core(h, shard, pred=True):
        pair = wbuf.at[h, pl.ds(4 * shard + 2 * c, 2)]
        send(CORE, pair, pair, s_wc.at[h, shard], r_wc.at[h, shard], pred)

    def w_own(h):
        for kind, q in ((UP, mine), (DOWN, mine), (SIDE, mine), (SIDE, theirs)):
            i = 4 * f + q
            src = w_hbm.at[q, :, pl.ds(h * wcols, wcols)]
            send(kind, src, wbuf.at[h, i], s_w.at[h, kind, i], r_w.at[h, i])

    def w_line(h, d):
        for dd, s, zp in line:
            if dd == d:
                ok, i = inside(zp), 4 * (2 * zp + x) + mine
                w_wait(h, i, ok)
                for kind in (UP if s > 0 else DOWN, SIDE, TWIN):
                    w_send(h, kind, i, ok)

    def w_side(h, d):
        if d == 0:
            i = 4 * (2 * z + other_x) + mine
            w_wait(h, i)
            i = 4 * (2 * z + other_x) + theirs
            w_wait(h, i)
            for kind in (UP, DOWN):
                w_send(h, kind, i)
            w_core(h, 2 * z + other_x)
            return
        for dd, s, zp in line:
            if dd == d:
                ok, i = inside(zp), 4 * (2 * zp + other_x) + mine
                w_wait(h, i, ok)
                if d > 1:
                    w_send(h, TWIN, i, ok)

    def w_twin(h, d, xx):
        for dd, s, zp in line:
            if dd == d:
                ok, i = inside(zp), 4 * (2 * zp + xx) + theirs
                w_wait(h, i, ok)
                w_core(h, 2 * zp + xx, ok)

    def shards(d):
        if d == 0:
            return [(True, f), (True, 2 * z + other_x)]
        return [(inside(zp), 2 * zp + xx) for dd, s, zp in line if dd == d for xx in (x, other_x)]

    def run(pred, step):
        if pred is True:
            step()
        else:
            pl.when(pred)(step)

    def add_base(h, d):
        for n, (ok, shard) in enumerate(shards(d)):
            def step(n=n, shard=shard):
                if d or n:
                    arrived(wbuf.at[h, pl.ds(4 * shard + 2 * other_c, 2)], r_wc.at[h, shard])
                weight = wbuf[h, pl.ds(4 * shard, 4)].reshape(part, wcols)
                both = xs[pl.ds(0, rows + BLOCK), lanes(shard * part, part)]
                base[:, h * wcols:(h + 1) * wcols] += dot(both, weight)

            run(ok, step)

    def train_probs(b):
        first = max(b - 1, 0) * BLOCK
        position_q = b * BLOCK + lax.broadcasted_iota(jnp.int32, (BLOCK, WINDOW), 0)
        position_k = first + lax.broadcasted_iota(jnp.int32, (BLOCK, WINDOW), 1)
        same = seg_col[pl.ds(b * BLOCK, BLOCK), :] == seg[...].astype(F32)[:, first:first + WINDOW]
        allowed = (position_k <= position_q) & same

        def head_group(g, _):
            q = stack_heads(qs, pl.ds(b * BLOCK, BLOCK), g)
            k = ks[pl.ds(first, WINDOW), lanes(g * HEAD_DIM, HEAD_DIM)]
            probs[b * KV_HEADS + g] = softmax_rows(nt_dot(q, k), allowed)
            return 0

        lax.fori_loop(0, KV_HEADS, head_group, 0)

    def score_probs():
        order_q = lax.broadcasted_iota(jnp.int32, (BLOCK, BLOCK), 0)
        order_k = lax.broadcasted_iota(jnp.int32, (BLOCK, BLOCK), 1)
        ids = sseg[...].astype(F32)
        column = jnp.broadcast_to(jnp.concatenate([ids, ids], axis=1), (WINDOW, WINDOW)).T
        allowed = (order_k <= order_q) & (column[:BLOCK, :BLOCK] == ids)

        def head_group(g, _):
            q = stack_heads(sq, pl.ds(0, BLOCK), g)
            sprobs[g] = softmax_rows(nt_dot(q, sk[:, lanes(g * HEAD_DIM, HEAD_DIM)]), allowed)
            return 0

        lax.fori_loop(0, KV_HEADS, head_group, 0)

    def low_step(i, acc):
        return acc + nt_dot(xs[pl.ds(0, rows), lanes(i * half, half)], dbuf[i])

    def attention(h):
        halves = pl.ds(h * wcols, wcols)
        up_half = up_ref[:, halves].astype(BF16)
        mixed = adapter_scale_factor * dot(low_s[...], up_half)
        vals[:, halves] = (base[pl.ds(0, rows), halves] + mixed).astype(BF16)
        for b in range(rows // BLOCK):
            first = max(b - 1, 0) * BLOCK

            def head_group(g, _, b=b, first=first):
                p = probs[b * KV_HEADS + g]
                cols = lanes(g * HEAD_DIM, HEAD_DIM)
                attended = dot(p, vals[pl.ds(first, WINDOW), cols])
                d_out = (attended - stack_heads(goal, pl.ds(b * BLOCK, BLOCK), g).astype(F32)).astype(BF16)
                dvals[pl.ds(first, WINDOW), cols] += tn_dot(p, d_out)
                return 0

            lax.fori_loop(h * KV_HEADS // 2, (h + 1) * KV_HEADS // 2, head_group, 0)

    sx_other = xs.at[pl.ds(rows + BLOCK, BLOCK)]
    dset = (dbuf, s_d, r_d)
    pieces_own(*dset)
    w_own(0)
    base[...] = jnp.zeros_like(base)
    dvals[...] = jnp.zeros_like(dvals)
    for i in range(1, 4):
        loads[i].wait()
    seg_col[...] = jnp.broadcast_to(seg[...].astype(F32), (WINDOW, rows)).T
    train_probs(0)
    pieces_line(*dset, 1)
    w_line(0, 1)
    pieces_side(*dset, 0)
    w_side(0, 0)
    w_own(1)
    send(CORE, sx_hbm, sx_other, s_sx, r_sx)
    train_probs(1)
    pieces_line(*dset, 2)
    w_line(0, 2)
    pieces_side(*dset, 1)
    w_side(0, 1)
    w_twin(0, 1, x)
    w_twin(0, 1, other_x)
    train_probs(2)
    pieces_line(*dset, 3)
    w_line(0, 3)
    pieces_side(*dset, 2)
    w_side(0, 2)
    w_twin(0, 2, x)
    w_line(1, 1)
    w_side(1, 0)
    train_probs(3)
    pieces_side(*dset, 3)
    w_side(0, 3)
    w_twin(0, 2, other_x)
    w_twin(0, 3, x)
    w_line(1, 2)
    w_side(1, 1)
    for i in range(4, len(loads)):
        loads[i].wait()
    score_probs()
    w_twin(1, 1, x)
    w_twin(1, 1, other_x)
    w_line(1, 3)
    w_twin(0, 3, other_x)
    pieces_core(dbuf, r_d)
    low = lax.fori_loop(0, 2 * N, low_step, jnp.zeros((rows, low_s.shape[1]), F32)).astype(BF16)
    low_s[...] = low
    w_side(1, 2)
    w_twin(1, 2, x)
    for d in range(DEPTH):
        add_base(0, d)
    w_side(1, 3)
    w_twin(1, 2, other_x)
    w_twin(1, 3, x)
    attention(0)
    w_twin(1, 3, other_x)
    for d in range(DEPTH):
        add_base(1, d)
    attention(1)
    up_half = up_ref[...].astype(BF16)
    dv = dvals[...].astype(BF16)
    dlow_t = (adapter_scale_factor * nt_dot(up_half, dv)).astype(BF16)

    def grad_of(peer, side):
        return dot(dlow_t, xs[pl.ds(0, rows), lanes(peer * part + side * half, half)])

    turns = [lax.rem(z + k, DEPTH) for k in range(1, DEPTH)] + [z]
    order = [2 * zt + xx for zt in turns for xx in (other_x, x)]
    for n, peer in enumerate(order):
        gsend[n] = grad_of(peer, other_c).astype(BF16)
        send(CORE, gsend.at[n], gpair.at[n], s_gp.at[n], r_gp.at[n])
    gu[...] = adapter_scale_factor * tn_dot(low_s[...], dv)
    ucols = VALUE_WIDTH // 2
    send(CORE, gu.at[:, lanes(other_c * ucols, ucols)], gupair, s_up, r_up)

    def core_sum(n):
        mine_of = grad_of(order[n], c)
        arrived(gpair.at[n], r_gp.at[n])
        return mine_of + gpair[n].astype(F32)

    for k in range(DEPTH):
        rsend[k] = core_sum(2 * k).astype(BF16)
        send(SIDE, rsend.at[k], rside.at[k], s_rx.at[k], r_rx.at[k])
    arrived(gupair, r_up)
    gusum[...] = gu[:, lanes(c * ucols, ucols)] + gupair[...]
    send(SIDE, gusum, guside, s_ur, r_ur)
    for k in range(DEPTH):
        total = core_sum(2 * k + 1)
        arrived(rside.at[k], r_rx.at[k])
        total = total + rside[k].astype(F32)
        if k < DEPTH - 1:
            rline[k] = total.astype(BF16)
            peer_send(2 * turns[k] + x, rline.at[k], rrecv.at[k], s_rs.at[k], r_rs.at[k])
    arrived(guside, r_ur)
    guline[z] = (gusum[...] + guside[...]).astype(BF16)
    flush()
    for k in range(DEPTH - 1):
        arrived(rrecv.at[k], r_rs.at[k])
        total = total + rrecv[k].astype(F32)
    new_half = down_t[:, lanes(c * half, half)] - rate_down * total
    ndbuf[f] = new_half.astype(BF16)
    for k in range(DEPTH - 1):
        peer_send(2 * turns[k] + x, ndbuf.at[f], ndbuf.at[f], s_nd.at[k], r_nd.at[f])
    send(SIDE, ndbuf.at[f], ndbuf.at[f], s_nd.at[DEPTH - 1], r_nd.at[f])
    for k in range(DEPTH - 1):
        peer_send(2 * turns[k] + x, guline.at[z], guline.at[z], s_ua.at[k], r_ua.at[z])
    fhalf[...] = new_half
    send(CORE, fhalf, frecv, s_f, r_f)

    def slow_of(shard):
        cols = lanes(shard * part + c * half, half)
        return nt_dot(xs[pl.ds(rows, 2 * BLOCK), cols], ndbuf[shard])

    arrived(sx_other, r_sx)
    slow = slow_of(f)
    for k in range(DEPTH - 1):
        shard = 2 * turns[k] + x
        arrived(ndbuf.at[shard], r_nd.at[shard])
        send(SIDE, ndbuf.at[shard], ndbuf.at[shard], s_nd.at[DEPTH + k], r_nd.at[shard])
    for k in range(DEPTH - 1):
        slow = slow + slow_of(2 * turns[k] + x)
        arrived(guline.at[turns[k]], r_ua.at[turns[k]])
    utotal = guline[0].astype(F32)
    for k in range(1, DEPTH):
        utotal = utotal + guline[k].astype(F32)
    guall[c] = utotal
    send(CORE, guall.at[c], guall.at[c], s_uc, r_uc)
    arrived(frecv, r_f)
    new_down_t[:, lanes(c * half, half)] = fhalf[...]
    new_down_t[:, lanes(other_c * half, half)] = frecv[...]
    for zt in [z] + turns[:-1]:
        shard = 2 * zt + other_x
        arrived(ndbuf.at[shard], r_nd.at[shard])
        slow = slow + slow_of(shard)
    slow_s[...] = slow
    send(CORE, slow_s.at[pl.ds(BLOCK, BLOCK)], slow_recv, s_sl, r_sl)
    arrived(guall.at[other_c], r_uc)
    for side in range(2):
        cols = pl.ds(side * ucols, ucols)
        new_up[:, cols] = up_ref[:, cols] - rate_up * guall[side]
    arrived(slow_recv, r_sl)
    slow = (slow_s[pl.ds(0, BLOCK), :] + slow_recv[...]).astype(BF16)
    svals = (
        base[pl.ds(rows, BLOCK), :] + adapter_scale_factor * dot(slow, new_up[...].astype(BF16))
    ).astype(BF16)
    for g in range(KV_HEADS):
        attended = dot(sprobs[g], svals[:, g * HEAD_DIM:(g + 1) * HEAD_DIM]).astype(BF16)
        for j in range(GROUP):
            at = (g * GROUP + j) * HEAD_DIM
            scored[:, at:at + HEAD_DIM] = attended[j * BLOCK:(j + 1) * BLOCK]

    flush()


def fused_body(
    train_input, train_query, train_keys, train_target, train_segments, value_weight, adapter_down, adapter_up,
    score_input, score_query, score_keys, score_segments,
):
    rows, width = train_input.shape[1:]
    part, rank = adapter_down.shape
    half = part // 2
    heads = train_query.shape[2]
    srows = score_input.shape[1]
    vw = value_weight.shape[1]
    hbm, vmem = pl.BlockSpec(memory_space=pltpu.HBM), pl.BlockSpec(memory_space=pltpu.VMEM)
    sem = pltpu.SemaphoreType.DMA
    uc = vw // 2
    piece = (rank, half)
    scratch = [
        pltpu.VMEM((rows + 2 * srows, width), BF16),
        pltpu.VMEM((rows, heads), BF16),
        pltpu.VMEM((rows, vw), BF16),
        pltpu.VMEM((rows, heads), BF16),
        pltpu.VMEM((1, rows), jnp.int32),
        pltpu.VMEM((rank, part), F32),
        pltpu.VMEM((rank, vw), F32),
        pltpu.VMEM((srows, heads), BF16),
        pltpu.VMEM((srows, vw), BF16),
        pltpu.VMEM((1, srows), jnp.int32),
        pltpu.VMEM((rows, WINDOW), F32),
        pltpu.VMEM((2, 4 * N, part // 4, vw // 2), BF16),
        pltpu.VMEM((2 * N, *piece), BF16),
        pltpu.VMEM((N, *piece), BF16),
        pltpu.VMEM((rows // BLOCK * KV_HEADS, GROUP * BLOCK, WINDOW), BF16),
        pltpu.VMEM((KV_HEADS, GROUP * BLOCK, BLOCK), BF16),
        pltpu.VMEM((rows + srows, vw), F32),
        pltpu.VMEM((rows, vw), BF16),
        pltpu.VMEM((rows, vw), F32),
        pltpu.VMEM((rows, rank), BF16),
        pltpu.VMEM((2 * srows, rank), F32),
        pltpu.VMEM((srows, rank), F32),
        pltpu.VMEM((N, *piece), BF16),
        pltpu.VMEM((N, *piece), BF16),
        pltpu.VMEM((DEPTH, *piece), BF16),
        pltpu.VMEM((DEPTH, *piece), BF16),
        pltpu.VMEM((DEPTH - 1, *piece), BF16),
        pltpu.VMEM((DEPTH - 1, *piece), BF16),
        pltpu.VMEM(piece, F32),
        pltpu.VMEM(piece, F32),
        pltpu.VMEM((rank, vw), F32),
        pltpu.VMEM((rank, uc), F32),
        pltpu.VMEM((rank, uc), F32),
        pltpu.VMEM((rank, uc), F32),
        pltpu.VMEM((DEPTH, rank, uc), BF16),
        pltpu.VMEM((2, rank, uc), F32),
        sem((13,)),
        sem((2, 5, 4 * N)), sem((2, 4 * N)),
        sem((2, N)), sem((2, N)),
        sem((5, 2 * N)), sem((2 * N,)),
        sem((2 * DEPTH - 1,)), sem((N,)),
        sem((N,)), sem((N,)),
        sem((DEPTH,)), sem((DEPTH,)),
        sem((DEPTH - 1,)), sem((DEPTH - 1,)),
        sem, sem,
        sem, sem,
        sem, sem,
        sem((DEPTH - 1,)), sem((DEPTH,)),
        sem, sem,
        sem, sem,
        sem, sem,
    ]
    new_down_t, new_up, scored = pl.pallas_call(
        fused_kernel,
        out_shape=(
            jax.ShapeDtypeStruct((rank, part), F32),
            jax.ShapeDtypeStruct(adapter_up.shape, F32),
            jax.ShapeDtypeStruct((srows, heads), BF16),
        ),
        in_specs=[hbm] * 12,
        out_specs=(vmem, vmem, vmem),
        scratch_shapes=scratch,
        compiler_params=pltpu.CompilerParams(
            collective_id=0, has_side_effects=True, vmem_limit_bytes=56 * 1024 * 1024
        ),
        name="test_time_step",
    )(
        train_input[0], train_query[0], train_keys[0], train_target[0], train_segments.reshape(1, rows),
        value_weight.reshape(4, part // 4, vw), adapter_down.T, adapter_up,
        score_input[0], score_query[0], score_keys[0], score_segments.reshape(1, srows),
    )
    return (new_down_t.T, new_up, scored[None])


def solution(mesh):
    in_specs = (
        P(("task", "view"), "fsdp", None),
        P(("task", "view"), "fsdp", None),
        P(("task", "view"), "fsdp", None),
        P(("task", "view"), "fsdp", None),
        P(("task", "view"), "fsdp", None),
        P("fsdp", None),
        P(("task", "fsdp"), None),
        P("task", None),
        P(("task", "view"), "fsdp", None),
        P(("task", "view"), "fsdp", None),
        P(("task", "view"), "fsdp", None),
        P(("task", "view"), "fsdp", None),
    )
    out_specs = (P(("task", "fsdp"), None), P("task", None), P(("task", "view"), "fsdp", None))
    local = fused_body if (mesh.shape["fsdp"], mesh.shape["view"]) == (8, 2) else body
    return jax.shard_map(local, mesh=mesh, in_specs=in_specs, out_specs=out_specs, check_vma=False)
```

```python
import jax
import jax.numpy as jnp
from jax import lax
from jax.experimental import pallas as pl
from jax.experimental.pallas import tpu as pltpu
from jax.sharding import PartitionSpec as P

Q_HEADS = 32
KV_HEADS = 4
HEAD_DIM = 128
GROUP = 8
VALUE_WIDTH = 512


adapter_scale_factor = 0.5
rate_down = 2e-05
rate_up = 0.001


def attend_row(query, keyset, value_rows, segment):
    length = query.shape[0]
    query_heads = query.reshape(length, KV_HEADS, GROUP, HEAD_DIM)
    key_heads = keyset.reshape(length, KV_HEADS, HEAD_DIM)
    logits = jnp.einsum(
        "qgjd,kgd->gjqk", query_heads, key_heads, preferred_element_type=jnp.float32
    ) * HEAD_DIM ** (-0.5)
    positions = jnp.arange(length, dtype=jnp.int32)
    allowed = (positions[None, :] <= positions[:, None]) & (segment[:, None] == segment[None, :])
    logits = jnp.where(allowed, logits, -1e30)
    peak = jnp.max(logits, axis=-1, keepdims=True)
    weights = jnp.exp(logits - peak)
    probs = (weights / jnp.sum(weights, axis=-1, keepdims=True)).astype(jnp.bfloat16)
    value_heads = value_rows.reshape(length, KV_HEADS, HEAD_DIM)
    attended = jnp.einsum("gjqk,kgd->qgjd", probs, value_heads, preferred_element_type=jnp.float32)
    return (probs, attended.reshape(length, Q_HEADS * HEAD_DIM))


def values_grad(probs, d_out):
    length = d_out.shape[0]
    heads = d_out.reshape(length, KV_HEADS, GROUP, HEAD_DIM)
    summed = jnp.einsum("gjqk,qgjd->kgd", probs, heads, preferred_element_type=jnp.float32)
    return summed.reshape(length, VALUE_WIDTH).astype(jnp.bfloat16)


def add_pieces(rows_in, pieces):
    return (
        jnp.dot(rows_in, pieces[0], preferred_element_type=jnp.float32),
        jnp.dot(rows_in, pieces[1], preferred_element_type=jnp.float32),
    )


def body(
    train_input,
    train_query,
    train_keys,
    train_target,
    train_segments,
    value_weight,
    adapter_down,
    adapter_up,
    score_input,
    score_query,
    score_keys,
    score_segments,
):
    width = train_input.shape[-1]
    value_width = value_weight.shape[1]
    count_rows = train_segments.shape[0] * train_segments.shape[1]
    row_length = train_segments.shape[2]
    score_length = score_segments.shape[2]
    down_half = adapter_down.astype(jnp.bfloat16)
    upper_weight_half = adapter_up.astype(jnp.bfloat16)
    train_rows = train_input.reshape(-1, width)
    frozen_base_weight, low = add_pieces(
        train_rows,
        (
            lax.all_gather(value_weight, "fsdp", axis=0, tiled=True),
            lax.all_gather(down_half, "fsdp", axis=0, tiled=True),
        ),
    )
    lower_rank_half = low.astype(jnp.bfloat16)
    value_rows = (
        frozen_base_weight
        + adapter_scale_factor
        * jnp.dot(lower_rank_half, upper_weight_half, preferred_element_type=jnp.float32)
    ).astype(jnp.bfloat16)
    probs, attended = jax.vmap(attend_row)(
        train_query,
        train_keys,
        value_rows.reshape(count_rows, row_length, -1),
        train_segments.reshape(count_rows, row_length),
    )
    d_out = (attended - train_target.astype(jnp.float32)).astype(jnp.bfloat16)
    value_output_gradient = jax.vmap(values_grad)(probs, d_out).reshape(-1, value_width)
    low_rank_gradient = (
        adapter_scale_factor
        * lax.dot_general(
            value_output_gradient,
            upper_weight_half,
            (((1,), (1,)), ((), ())),
            preferred_element_type=jnp.float32,
        )
    ).astype(jnp.bfloat16)
    local_up_gradient = adapter_scale_factor * lax.dot_general(
        lower_rank_half,
        value_output_gradient,
        (((0,), (0,)), ((), ())),
        preferred_element_type=jnp.float32,
    )
    grad_down = lax.psum_scatter(
        lax.dot_general(
            train_rows,
            low_rank_gradient,
            (((0,), (0,)), ((), ())),
            preferred_element_type=jnp.float32,
        ),
        "fsdp",
        scatter_dimension=0,
        tiled=True,
    )
    grad_down = lax.psum(grad_down, "view")
    up_weight_gradient = lax.psum(local_up_gradient, ("fsdp", "view"))
    new_down = adapter_down - rate_down * grad_down
    new_up = adapter_up - rate_up * up_weight_gradient
    new_down_half = new_down.astype(jnp.bfloat16)
    new_up_half = new_up.astype(jnp.bfloat16)
    score_rows = score_input.reshape(-1, width)
    score_base, score_low = add_pieces(
        score_rows,
        (
            lax.all_gather(value_weight, "fsdp", axis=0, tiled=True),
            lax.all_gather(new_down_half, "fsdp", axis=0, tiled=True),
        ),
    )
    score_values = (
        score_base
        + adapter_scale_factor
        * jnp.dot(score_low.astype(jnp.bfloat16), new_up_half, preferred_element_type=jnp.float32)
    ).astype(jnp.bfloat16)
    score_probs, score_attended = jax.vmap(attend_row)(
        score_query,
        score_keys,
        score_values.reshape(count_rows, score_length, -1),
        score_segments.reshape(count_rows, score_length),
    )
    scored = score_attended.astype(jnp.bfloat16)
    return (new_down, new_up, scored)


F32, BF16 = jnp.float32, jnp.bfloat16
N, DEPTH = 8, 4
BLOCK = 64
WINDOW = 2 * BLOCK
NT = (((1,), (1,)), ((), ()))
TN = (((0,), (0,)), ((), ()))
UP, DOWN, SIDE, TWIN, CORE = range(5)


def nt_dot(a, b):
    return lax.dot_general(a, b, NT, preferred_element_type=F32)


def tn_dot(a, b):
    return lax.dot_general(a, b, TN, preferred_element_type=F32)


def dot(a, b):
    return jnp.dot(a, b, preferred_element_type=F32)


def lanes(start, size):
    return pl.ds(pl.multiple_of(start, size), size)


def stack_heads(ref, rows, g):
    return jnp.concatenate(
        [ref[rows, lanes((g * GROUP + j) * HEAD_DIM, HEAD_DIM)] for j in range(GROUP)], axis=0
    )


def softmax_rows(logits, allowed):
    shape = logits.shape
    logits = (logits * HEAD_DIM ** (-0.5)).reshape(GROUP, BLOCK, shape[-1])
    logits = jnp.where(allowed[None], logits, -1e30)
    weights = jnp.exp(logits - jnp.max(logits, axis=-1, keepdims=True))
    probs = weights * (1.0 / jnp.sum(weights, axis=-1, keepdims=True))
    return probs.reshape(shape).astype(BF16)


def fused_kernel(
    x_hbm, q_hbm, k_hbm, goal_hbm, seg_hbm, w_hbm, down_hbm, up_hbm, sx_hbm, sq_hbm, sk_hbm, sseg_hbm,
    new_down_t, new_up, scored,
    xs, qs, ks, goal, seg, down_t, up_ref, sq, sk, sseg, seg_col, wbuf, dbuf, ndbuf, probs, sprobs, base, vals, dvals,
    low_s, slow_s, slow_recv, gsend, gpair, rsend, rside, rline, rrecv, fhalf, frecv,
    gu, gupair, gusum, guside, guline, guall,
    s_loc, s_w, s_wz, r_w, s_wc, r_wc, s_d, s_dz, r_d, s_nd, r_nd, s_gp, r_gp, s_rx, r_rx, s_rs, r_rs, s_f, r_f,
    s_up, r_up, s_ur, r_ur, s_ua, r_ua, s_uc, r_uc, s_sx, r_sx, s_sl, r_sl,
):
    t, f, c = lax.axis_index("task"), lax.axis_index("fsdp"), lax.axis_index("view")
    z, x = lax.div(f, 2), lax.rem(f, 2)
    other_t, other_x, other_c = 1 - t, 1 - x, 1 - c
    width = xs.shape[1]
    part = width // N
    half = part // 2
    rows = vals.shape[0]
    late = []
    wcols = VALUE_WIDTH // 2

    def device(kind):
        return {
            UP: {"fsdp": f + 2},
            DOWN: {"fsdp": f - 2},
            SIDE: {"fsdp": 2 * z + other_x},
            TWIN: {"task": other_t},
            CORE: {"view": other_c},
        }[kind]

    def exists(kind):
        return {UP: z < DEPTH - 1, DOWN: z > 0}.get(kind, True)

    def start(make, pred=True):
        if pred is True:
            make().start()
        else:
            pl.when(pred)(lambda: make().start())
        late.append((make, pred))

    def send(kind, src, dst, s_sem, r_sem, pred=True):
        where = exists(kind)
        if where is not True:
            pred = where if pred is True else jnp.logical_and(where, pred)

        def make():
            return pltpu.make_async_remote_copy(
                src_ref=src, dst_ref=dst, send_sem=s_sem, recv_sem=r_sem,
                device_id=device(kind), device_id_type=pl.DeviceIdType.MESH,
            )

        start(make, pred)

    def peer_send(peer, src, dst, s_sem, r_sem):
        def make():
            return pltpu.make_async_remote_copy(
                src_ref=src, dst_ref=dst, send_sem=s_sem, recv_sem=r_sem,
                device_id={"fsdp": peer}, device_id_type=pl.DeviceIdType.MESH,
            )

        start(make)

    def arrived(dst, r_sem, pred=True):
        def wait():
            pltpu.make_async_remote_copy(
                src_ref=dst, dst_ref=dst, send_sem=r_sem, recv_sem=r_sem,
                device_id={"view": other_c}, device_id_type=pl.DeviceIdType.MESH,
            ).wait_recv()

        if pred is True:
            wait()
        else:
            pl.when(pred)(wait)

    def flush():
        def finish(make):
            make().wait_send()

        for make, pred in late:
            if pred is True:
                finish(make)
            else:
                pl.when(pred)(lambda make=make: finish(make))
        late.clear()

    def peers():
        return [lax.rem(f + k, N) for k in range(1, N)]

    barrier = pltpu.get_barrier_semaphore()
    for peer in peers():
        pl.semaphore_signal(barrier, inc=1, device_id={"fsdp": peer}, device_id_type=pl.DeviceIdType.MESH)
    for kind in (TWIN, CORE):
        pl.semaphore_signal(barrier, inc=1, device_id=device(kind), device_id_type=pl.DeviceIdType.MESH)

    local = [
        (down_hbm, down_t),
        (q_hbm, qs),
        (k_hbm, ks),
        (seg_hbm, seg),
        (sq_hbm, sq),
        (sk_hbm, sk),
        (sseg_hbm, sseg),
        (x_hbm, xs.at[pl.ds(0, rows)]),
        (sx_hbm, xs.at[pl.ds(rows, BLOCK)]),
        (up_hbm, up_ref),
        (goal_hbm, goal),
    ] + [(w_hbm.at[:, :, pl.ds(h * wcols, wcols)], wbuf.at[h, pl.ds(4 * f, 4)]) for h in range(2)]
    loads = [pltpu.make_async_copy(a, b, s_loc.at[i]) for i, (a, b) in enumerate(local)]
    for load in loads:
        load.start()
    loads[0].wait()
    for side in range(2):
        dbuf[2 * f + side] = down_t[:, side * half:(side + 1) * half].astype(BF16)
    pl.semaphore_wait(barrier, N + 1)

    to_turn = [lax.rem(z + k, DEPTH) for k in range(1, DEPTH)]
    from_turn = [lax.rem(z + DEPTH - k, DEPTH) for k in range(1, DEPTH)]

    def d_own():
        i = 2 * f + c
        send(SIDE, dbuf.at[i], dbuf.at[i], s_d.at[SIDE, i], r_d.at[i])
        for k, zt in enumerate(to_turn):
            peer_send(2 * zt + x, dbuf.at[i], dbuf.at[i], s_dz.at[k], r_d.at[i])

    def d_line(k):
        i = 2 * (2 * from_turn[k] + x) + c
        arrived(dbuf.at[i], r_d.at[i])
        for kind in (SIDE, CORE):
            send(kind, dbuf.at[i], dbuf.at[i], s_d.at[kind, i], r_d.at[i])

    def d_side():
        for zt in [z] + from_turn:
            i = 2 * (2 * zt + other_x) + c
            arrived(dbuf.at[i], r_d.at[i])
            send(CORE, dbuf.at[i], dbuf.at[i], s_d.at[CORE, i], r_d.at[i])

    def d_core():
        for peer in peers():
            i = 2 * peer + other_c
            arrived(dbuf.at[i], r_d.at[i])

    mine, theirs = 2 * c + t, 2 * c + other_t

    def w_send(h, kind, i, pred=True):
        send(kind, wbuf.at[h, i], wbuf.at[h, i], s_w.at[h, kind, i], r_w.at[h, i], pred)

    def w_wait(h, i):
        arrived(wbuf.at[h, i], r_w.at[h, i])

    def w_core(h, shard):
        pair = wbuf.at[h, pl.ds(4 * shard + 2 * c, 2)]
        send(CORE, pair, pair, s_wc.at[h, shard], r_wc.at[h, shard])

    def w_own(h):
        cols = pl.ds(h * wcols, wcols)
        for q in (mine, theirs):
            i = 4 * f + q
            send(SIDE, w_hbm.at[q, :, cols], wbuf.at[h, i], s_w.at[h, SIDE, i], r_w.at[h, i])
        i = 4 * f + mine
        for k, zt in enumerate(to_turn):
            peer_send(2 * zt + x, w_hbm.at[mine, :, cols], wbuf.at[h, i], s_wz.at[h, k], r_w.at[h, i])

    def w_line(h, k):
        i = 4 * (2 * from_turn[k] + x) + mine
        w_wait(h, i)
        for kind in (SIDE, TWIN):
            w_send(h, kind, i)

    def w_side_own(h):
        shard = 2 * z + other_x
        w_wait(h, 4 * shard + mine)
        w_wait(h, 4 * shard + theirs)
        for kind in (UP, DOWN):
            w_send(h, kind, 4 * shard + theirs)
        w_core(h, shard)

    def w_side(h, k):
        zt = from_turn[k]
        i = 4 * (2 * zt + other_x) + mine
        w_wait(h, i)
        w_send(h, TWIN, i, jnp.logical_and(zt - z != 1, z - zt != 1))

    def w_twin(h, k, xx):
        shard = 2 * from_turn[k] + xx
        w_wait(h, 4 * shard + theirs)
        w_core(h, shard)

    def add_base(h):
        shards = [2 * zt + xx for zt in [z] + from_turn for xx in (x, other_x)]
        for n, shard in enumerate(shards):
            if n:
                arrived(wbuf.at[h, pl.ds(4 * shard + 2 * other_c, 2)], r_wc.at[h, shard])
            weight = wbuf[h, pl.ds(4 * shard, 4)].reshape(part, wcols)
            both = xs[pl.ds(0, rows + BLOCK), lanes(shard * part, part)]
            base[:, h * wcols:(h + 1) * wcols] += dot(both, weight)

    def train_probs(step):
        b, pair = step // 2, step % 2
        first = max(b - 1, 0) * BLOCK
        position_q = b * BLOCK + lax.broadcasted_iota(jnp.int32, (BLOCK, WINDOW), 0)
        position_k = first + lax.broadcasted_iota(jnp.int32, (BLOCK, WINDOW), 1)
        same = seg_col[pl.ds(b * BLOCK, BLOCK), :] == seg[...].astype(F32)[:, first:first + WINDOW]
        allowed = (position_k <= position_q) & same

        def head_group(g, _):
            q = stack_heads(qs, pl.ds(b * BLOCK, BLOCK), g)
            k = ks[pl.ds(first, WINDOW), lanes(g * HEAD_DIM, HEAD_DIM)]
            probs[b * KV_HEADS + g] = softmax_rows(nt_dot(q, k), allowed)
            return 0

        lax.fori_loop(pair * KV_HEADS // 2, (pair + 1) * KV_HEADS // 2, head_group, 0)

    def score_probs():
        order_q = lax.broadcasted_iota(jnp.int32, (BLOCK, BLOCK), 0)
        order_k = lax.broadcasted_iota(jnp.int32, (BLOCK, BLOCK), 1)
        ids = sseg[...].astype(F32)
        column = jnp.broadcast_to(jnp.concatenate([ids, ids], axis=1), (WINDOW, WINDOW)).T
        allowed = (order_k <= order_q) & (column[:BLOCK, :BLOCK] == ids)

        def head_group(g, _):
            q = stack_heads(sq, pl.ds(0, BLOCK), g)
            sprobs[g] = softmax_rows(nt_dot(q, sk[:, lanes(g * HEAD_DIM, HEAD_DIM)]), allowed)
            return 0

        lax.fori_loop(0, KV_HEADS, head_group, 0)

    def low_step(i, acc):
        return acc + nt_dot(xs[pl.ds(0, rows), lanes(i * half, half)], dbuf[i])

    def attention(h):
        halves = pl.ds(h * wcols, wcols)
        up_half = up_ref[:, halves].astype(BF16)
        mixed = adapter_scale_factor * dot(low_s[...], up_half)
        vals[:, halves] = (base[pl.ds(0, rows), halves] + mixed).astype(BF16)
        for b in range(rows // BLOCK):
            first = max(b - 1, 0) * BLOCK

            def head_group(g, _, b=b, first=first):
                p = probs[b * KV_HEADS + g]
                cols = lanes(g * HEAD_DIM, HEAD_DIM)
                attended = dot(p, vals[pl.ds(first, WINDOW), cols])
                d_out = (attended - stack_heads(goal, pl.ds(b * BLOCK, BLOCK), g).astype(F32)).astype(BF16)
                dvals[pl.ds(first, WINDOW), cols] += tn_dot(p, d_out)
                return 0

            lax.fori_loop(h * KV_HEADS // 2, (h + 1) * KV_HEADS // 2, head_group, 0)

    sx_other = xs.at[pl.ds(rows + BLOCK, BLOCK)]
    d_own()
    w_own(0)
    base[...] = jnp.zeros_like(base)
    dvals[...] = jnp.zeros_like(dvals)
    for i in range(1, 4):
        loads[i].wait()
    seg_col[...] = jnp.broadcast_to(seg[...].astype(F32), (WINDOW, rows)).T
    train_probs(0)
    w_side_own(0)
    w_line(0, 0)
    train_probs(1)
    w_line(0, 1)
    w_own(1)
    send(CORE, sx_hbm, sx_other, s_sx, r_sx)
    train_probs(2)
    w_line(0, 2)
    for k in range(DEPTH - 1):
        d_line(k)
    train_probs(3)
    w_side(0, 0)
    w_twin(0, 0, x)
    train_probs(4)
    w_side_own(1)
    w_line(1, 0)
    w_side(0, 1)
    w_twin(0, 1, x)
    train_probs(5)
    w_line(1, 1)
    w_side(0, 2)
    w_twin(0, 2, x)
    train_probs(6)
    w_line(1, 2)
    d_side()
    w_twin(0, 0, other_x)
    w_twin(0, 1, other_x)
    train_probs(7)
    w_side(1, 0)
    w_twin(1, 0, x)
    for i in range(4, len(loads)):
        loads[i].wait()
    score_probs()
    w_twin(0, 2, other_x)
    w_side(1, 1)
    w_twin(1, 1, x)
    d_core()
    low = lax.fori_loop(0, 2 * N, low_step, jnp.zeros((rows, low_s.shape[1]), F32)).astype(BF16)
    low_s[...] = low
    w_side(1, 2)
    w_twin(1, 2, x)
    add_base(0)
    w_twin(1, 0, other_x)
    w_twin(1, 1, other_x)
    attention(0)
    w_twin(1, 2, other_x)
    add_base(1)
    attention(1)
    up_half = up_ref[...].astype(BF16)
    dv = dvals[...].astype(BF16)
    dlow_t = (adapter_scale_factor * nt_dot(up_half, dv)).astype(BF16)

    def grad_of(peer, side):
        return dot(dlow_t, xs[pl.ds(0, rows), lanes(peer * part + side * half, half)])

    turns = to_turn + [z]
    order = [2 * zt + xx for zt in turns for xx in (other_x, x)]
    for n, peer in enumerate(order):
        gsend[n] = grad_of(peer, other_c).astype(BF16)
        send(CORE, gsend.at[n], gpair.at[n], s_gp.at[n], r_gp.at[n])
    gu[...] = adapter_scale_factor * tn_dot(low_s[...], dv)
    ucols = VALUE_WIDTH // 2
    send(CORE, gu.at[:, lanes(other_c * ucols, ucols)], gupair, s_up, r_up)

    def core_sum(n):
        mine_of = grad_of(order[n], c)
        arrived(gpair.at[n], r_gp.at[n])
        return mine_of + gpair[n].astype(F32)

    for k in range(DEPTH):
        rsend[k] = core_sum(2 * k).astype(BF16)
        send(SIDE, rsend.at[k], rside.at[k], s_rx.at[k], r_rx.at[k])
    arrived(gupair, r_up)
    gusum[...] = gu[:, lanes(c * ucols, ucols)] + gupair[...]
    send(SIDE, gusum, guside, s_ur, r_ur)
    for k in range(DEPTH):
        total = core_sum(2 * k + 1)
        arrived(rside.at[k], r_rx.at[k])
        total = total + rside[k].astype(F32)
        if k < DEPTH - 1:
            rline[k] = total.astype(BF16)
            peer_send(2 * turns[k] + x, rline.at[k], rrecv.at[k], s_rs.at[k], r_rs.at[k])
    arrived(guside, r_ur)
    guline[z] = (gusum[...] + guside[...]).astype(BF16)
    flush()
    for k in range(DEPTH - 1):
        arrived(rrecv.at[k], r_rs.at[k])
        total = total + rrecv[k].astype(F32)
    new_half = down_t[:, lanes(c * half, half)] - rate_down * total
    ndbuf[f] = new_half.astype(BF16)
    for k in range(DEPTH - 1):
        peer_send(2 * turns[k] + x, ndbuf.at[f], ndbuf.at[f], s_nd.at[k], r_nd.at[f])
    send(SIDE, ndbuf.at[f], ndbuf.at[f], s_nd.at[DEPTH - 1], r_nd.at[f])
    for k in range(DEPTH - 1):
        peer_send(2 * turns[k] + x, guline.at[z], guline.at[z], s_ua.at[k], r_ua.at[z])
    fhalf[...] = new_half
    send(CORE, fhalf, frecv, s_f, r_f)

    def slow_of(shard):
        cols = lanes(shard * part + c * half, half)
        return nt_dot(xs[pl.ds(rows, 2 * BLOCK), cols], ndbuf[shard])

    arrived(sx_other, r_sx)
    slow = slow_of(f)
    for k in range(DEPTH - 1):
        shard = 2 * from_turn[k] + x
        arrived(ndbuf.at[shard], r_nd.at[shard])
        send(SIDE, ndbuf.at[shard], ndbuf.at[shard], s_nd.at[DEPTH + k], r_nd.at[shard])
    for k in range(DEPTH - 1):
        slow = slow + slow_of(2 * from_turn[k] + x)
        arrived(guline.at[from_turn[k]], r_ua.at[from_turn[k]])
    utotal = guline[0].astype(F32)
    for k in range(1, DEPTH):
        utotal = utotal + guline[k].astype(F32)
    guall[c] = utotal
    send(CORE, guall.at[c], guall.at[c], s_uc, r_uc)
    arrived(frecv, r_f)
    new_down_t[:, lanes(c * half, half)] = fhalf[...]
    new_down_t[:, lanes(other_c * half, half)] = frecv[...]
    for zt in [z] + from_turn:
        shard = 2 * zt + other_x
        arrived(ndbuf.at[shard], r_nd.at[shard])
        slow = slow + slow_of(shard)
    slow_s[...] = slow
    send(CORE, slow_s.at[pl.ds(BLOCK, BLOCK)], slow_recv, s_sl, r_sl)
    arrived(guall.at[other_c], r_uc)
    for side in range(2):
        cols = pl.ds(side * ucols, ucols)
        new_up[:, cols] = up_ref[:, cols] - rate_up * guall[side]
    arrived(slow_recv, r_sl)
    slow = (slow_s[pl.ds(0, BLOCK), :] + slow_recv[...]).astype(BF16)
    svals = (
        base[pl.ds(rows, BLOCK), :] + adapter_scale_factor * dot(slow, new_up[...].astype(BF16))
    ).astype(BF16)
    for g in range(KV_HEADS):
        attended = dot(sprobs[g], svals[:, g * HEAD_DIM:(g + 1) * HEAD_DIM]).astype(BF16)
        for j in range(GROUP):
            at = (g * GROUP + j) * HEAD_DIM
            scored[:, at:at + HEAD_DIM] = attended[j * BLOCK:(j + 1) * BLOCK]

    flush()


def hand_over(a, b, c, a_out, b_out, c_out, sems):
    copies = [
        pltpu.make_async_copy(src, dst, sems.at[i]) for i, (src, dst) in enumerate(((a, a_out), (b, b_out), (c, c_out)))
    ]
    for copy in copies:
        copy.start()
    for copy in copies:
        copy.wait()


def fused_body(
    train_input, train_query, train_keys, train_target, train_segments, value_weight, adapter_down, adapter_up,
    score_input, score_query, score_keys, score_segments,
):
    rows, width = train_input.shape[1:]
    part, rank = adapter_down.shape
    half = part // 2
    heads = train_query.shape[2]
    srows = score_input.shape[1]
    vw = value_weight.shape[1]
    hbm, vmem = pl.BlockSpec(memory_space=pltpu.HBM), pl.BlockSpec(memory_space=pltpu.VMEM)
    sem = pltpu.SemaphoreType.DMA
    uc = vw // 2
    piece = (rank, half)
    scratch = [
        pltpu.VMEM((rows + 2 * srows, width), BF16),
        pltpu.VMEM((rows, heads), BF16),
        pltpu.VMEM((rows, vw), BF16),
        pltpu.VMEM((rows, heads), BF16),
        pltpu.VMEM((1, rows), jnp.int32),
        pltpu.VMEM((rank, part), F32),
        pltpu.VMEM((rank, vw), F32),
        pltpu.VMEM((srows, heads), BF16),
        pltpu.VMEM((srows, vw), BF16),
        pltpu.VMEM((1, srows), jnp.int32),
        pltpu.VMEM((rows, WINDOW), F32),
        pltpu.VMEM((2, 4 * N, part // 4, vw // 2), BF16),
        pltpu.VMEM((2 * N, *piece), BF16),
        pltpu.VMEM((N, *piece), BF16),
        pltpu.VMEM((rows // BLOCK * KV_HEADS, GROUP * BLOCK, WINDOW), BF16),
        pltpu.VMEM((KV_HEADS, GROUP * BLOCK, BLOCK), BF16),
        pltpu.VMEM((rows + srows, vw), F32),
        pltpu.VMEM((rows, vw), BF16),
        pltpu.VMEM((rows, vw), F32),
        pltpu.VMEM((rows, rank), BF16),
        pltpu.VMEM((2 * srows, rank), F32),
        pltpu.VMEM((srows, rank), F32),
        pltpu.VMEM((N, *piece), BF16),
        pltpu.VMEM((N, *piece), BF16),
        pltpu.VMEM((DEPTH, *piece), BF16),
        pltpu.VMEM((DEPTH, *piece), BF16),
        pltpu.VMEM((DEPTH - 1, *piece), BF16),
        pltpu.VMEM((DEPTH - 1, *piece), BF16),
        pltpu.VMEM(piece, F32),
        pltpu.VMEM(piece, F32),
        pltpu.VMEM((rank, vw), F32),
        pltpu.VMEM((rank, uc), F32),
        pltpu.VMEM((rank, uc), F32),
        pltpu.VMEM((rank, uc), F32),
        pltpu.VMEM((DEPTH, rank, uc), BF16),
        pltpu.VMEM((2, rank, uc), F32),
        sem((13,)),
        sem((2, 5, 4 * N)), sem((2, DEPTH - 1)), sem((2, 4 * N)),
        sem((2, N)), sem((2, N)),
        sem((5, 2 * N)), sem((DEPTH - 1,)), sem((2 * N,)),
        sem((2 * DEPTH - 1,)), sem((N,)),
        sem((N,)), sem((N,)),
        sem((DEPTH,)), sem((DEPTH,)),
        sem((DEPTH - 1,)), sem((DEPTH - 1,)),
        sem, sem,
        sem, sem,
        sem, sem,
        sem((DEPTH - 1,)), sem((DEPTH,)),
        sem, sem,
        sem, sem,
        sem, sem,
    ]
    new_down_t, new_up, scored = pl.pallas_call(
        fused_kernel,
        out_shape=(
            jax.ShapeDtypeStruct((rank, part), F32),
            jax.ShapeDtypeStruct(adapter_up.shape, F32),
            jax.ShapeDtypeStruct((srows, heads), BF16),
        ),
        in_specs=[hbm] * 12,
        out_specs=(vmem, vmem, vmem),
        scratch_shapes=scratch,
        compiler_params=pltpu.CompilerParams(
            collective_id=0, has_side_effects=True, vmem_limit_bytes=56 * 1024 * 1024
        ),
        name="test_time_step",
    )(
        train_input[0], train_query[0], train_keys[0], train_target[0], train_segments.reshape(1, rows),
        value_weight.reshape(4, part // 4, vw), adapter_down.T, adapter_up,
        score_input[0], score_query[0], score_keys[0], score_segments.reshape(1, srows),
    )
    new_down_t, new_up, scored = pl.pallas_call(
        hand_over,
        out_shape=tuple(jax.ShapeDtypeStruct(a.shape, a.dtype) for a in (new_down_t, new_up, scored)),
        in_specs=[hbm] * 3,
        out_specs=(hbm,) * 3,
        scratch_shapes=[sem((3,))],
        compiler_params=pltpu.CompilerParams(vmem_limit_bytes=56 * 1024 * 1024),
        name="hand_over",
    )(new_down_t, new_up, scored)
    return (new_down_t.T, new_up, scored[None])


def solution(mesh):
    in_specs = (
        P(("task", "view"), "fsdp", None),
        P(("task", "view"), "fsdp", None),
        P(("task", "view"), "fsdp", None),
        P(("task", "view"), "fsdp", None),
        P(("task", "view"), "fsdp", None),
        P("fsdp", None),
        P(("task", "fsdp"), None),
        P("task", None),
        P(("task", "view"), "fsdp", None),
        P(("task", "view"), "fsdp", None),
        P(("task", "view"), "fsdp", None),
        P(("task", "view"), "fsdp", None),
    )
    out_specs = (P(("task", "fsdp"), None), P("task", None), P(("task", "view"), "fsdp", None))
    local = fused_body if (mesh.shape["fsdp"], mesh.shape["view"]) == (8, 2) else body
    return jax.shard_map(local, mesh=mesh, in_specs=in_specs, out_specs=out_specs, check_vma=False)
```

```python
import jax
import jax.numpy as jnp
from jax import lax
from jax.experimental import pallas as pl
from jax.experimental.pallas import tpu as pltpu
from jax.sharding import PartitionSpec as P

Q_HEADS = 32
KV_HEADS = 4
HEAD_DIM = 128
GROUP = 8
VALUE_WIDTH = 512


adapter_scale_factor = 0.5
rate_down = 2e-05
rate_up = 0.001


def attend_row(query, keyset, value_rows, segment):
    length = query.shape[0]
    query_heads = query.reshape(length, KV_HEADS, GROUP, HEAD_DIM)
    key_heads = keyset.reshape(length, KV_HEADS, HEAD_DIM)
    logits = jnp.einsum(
        "qgjd,kgd->gjqk", query_heads, key_heads, preferred_element_type=jnp.float32
    ) * HEAD_DIM ** (-0.5)
    positions = jnp.arange(length, dtype=jnp.int32)
    allowed = (positions[None, :] <= positions[:, None]) & (segment[:, None] == segment[None, :])
    logits = jnp.where(allowed, logits, -1e30)
    peak = jnp.max(logits, axis=-1, keepdims=True)
    weights = jnp.exp(logits - peak)
    probs = (weights / jnp.sum(weights, axis=-1, keepdims=True)).astype(jnp.bfloat16)
    value_heads = value_rows.reshape(length, KV_HEADS, HEAD_DIM)
    attended = jnp.einsum("gjqk,kgd->qgjd", probs, value_heads, preferred_element_type=jnp.float32)
    return (probs, attended.reshape(length, Q_HEADS * HEAD_DIM))


def values_grad(probs, d_out):
    length = d_out.shape[0]
    heads = d_out.reshape(length, KV_HEADS, GROUP, HEAD_DIM)
    summed = jnp.einsum("gjqk,qgjd->kgd", probs, heads, preferred_element_type=jnp.float32)
    return summed.reshape(length, VALUE_WIDTH).astype(jnp.bfloat16)


def add_pieces(rows_in, pieces):
    return (
        jnp.dot(rows_in, pieces[0], preferred_element_type=jnp.float32),
        jnp.dot(rows_in, pieces[1], preferred_element_type=jnp.float32),
    )


def body(
    train_input,
    train_query,
    train_keys,
    train_target,
    train_segments,
    value_weight,
    adapter_down,
    adapter_up,
    score_input,
    score_query,
    score_keys,
    score_segments,
):
    width = train_input.shape[-1]
    value_width = value_weight.shape[1]
    count_rows = train_segments.shape[0] * train_segments.shape[1]
    row_length = train_segments.shape[2]
    score_length = score_segments.shape[2]
    down_half = adapter_down.astype(jnp.bfloat16)
    upper_weight_half = adapter_up.astype(jnp.bfloat16)
    train_rows = train_input.reshape(-1, width)
    frozen_base_weight, low = add_pieces(
        train_rows,
        (
            lax.all_gather(value_weight, "fsdp", axis=0, tiled=True),
            lax.all_gather(down_half, "fsdp", axis=0, tiled=True),
        ),
    )
    lower_rank_half = low.astype(jnp.bfloat16)
    value_rows = (
        frozen_base_weight
        + adapter_scale_factor
        * jnp.dot(lower_rank_half, upper_weight_half, preferred_element_type=jnp.float32)
    ).astype(jnp.bfloat16)
    probs, attended = jax.vmap(attend_row)(
        train_query,
        train_keys,
        value_rows.reshape(count_rows, row_length, -1),
        train_segments.reshape(count_rows, row_length),
    )
    d_out = (attended - train_target.astype(jnp.float32)).astype(jnp.bfloat16)
    value_output_gradient = jax.vmap(values_grad)(probs, d_out).reshape(-1, value_width)
    low_rank_gradient = (
        adapter_scale_factor
        * lax.dot_general(
            value_output_gradient,
            upper_weight_half,
            (((1,), (1,)), ((), ())),
            preferred_element_type=jnp.float32,
        )
    ).astype(jnp.bfloat16)
    local_up_gradient = adapter_scale_factor * lax.dot_general(
        lower_rank_half,
        value_output_gradient,
        (((0,), (0,)), ((), ())),
        preferred_element_type=jnp.float32,
    )
    grad_down = lax.psum_scatter(
        lax.dot_general(
            train_rows,
            low_rank_gradient,
            (((0,), (0,)), ((), ())),
            preferred_element_type=jnp.float32,
        ),
        "fsdp",
        scatter_dimension=0,
        tiled=True,
    )
    grad_down = lax.psum(grad_down, "view")
    up_weight_gradient = lax.psum(local_up_gradient, ("fsdp", "view"))
    new_down = adapter_down - rate_down * grad_down
    new_up = adapter_up - rate_up * up_weight_gradient
    new_down_half = new_down.astype(jnp.bfloat16)
    new_up_half = new_up.astype(jnp.bfloat16)
    score_rows = score_input.reshape(-1, width)
    score_base, score_low = add_pieces(
        score_rows,
        (
            lax.all_gather(value_weight, "fsdp", axis=0, tiled=True),
            lax.all_gather(new_down_half, "fsdp", axis=0, tiled=True),
        ),
    )
    score_values = (
        score_base
        + adapter_scale_factor
        * jnp.dot(score_low.astype(jnp.bfloat16), new_up_half, preferred_element_type=jnp.float32)
    ).astype(jnp.bfloat16)
    score_probs, score_attended = jax.vmap(attend_row)(
        score_query,
        score_keys,
        score_values.reshape(count_rows, score_length, -1),
        score_segments.reshape(count_rows, score_length),
    )
    scored = score_attended.astype(jnp.bfloat16)
    return (new_down, new_up, scored)


F32, BF16 = jnp.float32, jnp.bfloat16
N, DEPTH = 8, 4
BLOCK = 64
WINDOW = 2 * BLOCK
NT = (((1,), (1,)), ((), ()))
TN = (((0,), (0,)), ((), ()))
UP, DOWN, SIDE, TWIN, CORE = range(5)


def nt_dot(a, b):
    return lax.dot_general(a, b, NT, preferred_element_type=F32)


def tn_dot(a, b):
    return lax.dot_general(a, b, TN, preferred_element_type=F32)


def dot(a, b):
    return jnp.dot(a, b, preferred_element_type=F32)


def lanes(start, size):
    return pl.ds(pl.multiple_of(start, size), size)


def stack_heads(ref, rows, g):
    return jnp.concatenate(
        [ref[rows, lanes((g * GROUP + j) * HEAD_DIM, HEAD_DIM)] for j in range(GROUP)], axis=0
    )


def softmax_rows(logits, allowed):
    shape = logits.shape
    logits = (logits * HEAD_DIM ** (-0.5)).reshape(GROUP, BLOCK, shape[-1])
    logits = jnp.where(allowed[None], logits, -1e30)
    weights = jnp.exp(logits - jnp.max(logits, axis=-1, keepdims=True))
    probs = weights * (1.0 / jnp.sum(weights, axis=-1, keepdims=True))
    return probs.reshape(shape).astype(BF16)


def fused_kernel(
    x_hbm, q_hbm, k_hbm, goal_hbm, seg_hbm, w_hbm, down_hbm, up_hbm, sx_hbm, sq_hbm, sk_hbm, sseg_hbm,
    new_down_t, new_up, scored,
    xs, qs, ks, goal, seg, down_t, up_ref, sq, sk, sseg, seg_col, wbuf, dbuf, ndbuf, probs, sprobs, base, vals, dvals,
    low_s, slow_s, slow_recv, gsend, gpair, rsend, rside, rline, rrecv, fhalf, frecv,
    gu, gupair, gusum, guside, guline, guall,
    s_loc, s_w, r_w, s_wc, r_wc, s_d, r_d, s_nd, r_nd, s_gp, r_gp, s_rx, r_rx, s_rs, r_rs, s_f, r_f,
    s_up, r_up, s_ur, r_ur, s_ua, r_ua, s_uc, r_uc, s_sx, r_sx, s_sl, r_sl,
):
    t, f, c = lax.axis_index("task"), lax.axis_index("fsdp"), lax.axis_index("view")
    z, x = lax.div(f, 2), lax.rem(f, 2)
    other_t, other_x, other_c = 1 - t, 1 - x, 1 - c
    width = xs.shape[1]
    part = width // N
    half = part // 2
    rows = vals.shape[0]
    late = []
    wcols = VALUE_WIDTH // 2

    def device(kind):
        return {
            UP: {"fsdp": f + 2},
            DOWN: {"fsdp": f - 2},
            SIDE: {"fsdp": 2 * z + other_x},
            TWIN: {"task": other_t},
            CORE: {"view": other_c},
        }[kind]

    def exists(kind):
        return {UP: z < DEPTH - 1, DOWN: z > 0}.get(kind, True)

    def start(make, pred=True):
        if pred is True:
            make().start()
        else:
            pl.when(pred)(lambda: make().start())
        late.append((make, pred))

    def send(kind, src, dst, s_sem, r_sem, pred=True):
        where = exists(kind)
        if where is not True:
            pred = where if pred is True else jnp.logical_and(where, pred)

        def make():
            return pltpu.make_async_remote_copy(
                src_ref=src, dst_ref=dst, send_sem=s_sem, recv_sem=r_sem,
                device_id=device(kind), device_id_type=pl.DeviceIdType.MESH,
            )

        start(make, pred)

    def peer_send(peer, src, dst, s_sem, r_sem):
        def make():
            return pltpu.make_async_remote_copy(
                src_ref=src, dst_ref=dst, send_sem=s_sem, recv_sem=r_sem,
                device_id={"fsdp": peer}, device_id_type=pl.DeviceIdType.MESH,
            )

        start(make)

    def arrived(dst, r_sem, pred=True):
        def wait():
            pltpu.make_async_remote_copy(
                src_ref=dst, dst_ref=dst, send_sem=r_sem, recv_sem=r_sem,
                device_id={"view": other_c}, device_id_type=pl.DeviceIdType.MESH,
            ).wait_recv()

        if pred is True:
            wait()
        else:
            pl.when(pred)(wait)

    def flush():
        def finish(make):
            make().wait_send()

        for make, pred in late:
            if pred is True:
                finish(make)
            else:
                pl.when(pred)(lambda make=make: finish(make))
        late.clear()

    def peers():
        return [lax.rem(f + k, N) for k in range(1, N)]

    barrier = pltpu.get_barrier_semaphore()
    for peer in peers():
        pl.semaphore_signal(barrier, inc=1, device_id={"fsdp": peer}, device_id_type=pl.DeviceIdType.MESH)
    for kind in (TWIN, CORE):
        pl.semaphore_signal(barrier, inc=1, device_id=device(kind), device_id_type=pl.DeviceIdType.MESH)

    local = [(down_hbm, down_t)]
    local += [(w_hbm.at[:, :, pl.ds(h * wcols, wcols)], wbuf.at[h, pl.ds(4 * f, 4)]) for h in range(2)]
    local += [
        (q_hbm, qs),
        (k_hbm, ks),
        (seg_hbm, seg),
        (sx_hbm, xs.at[pl.ds(rows, BLOCK)]),
        (sq_hbm, sq),
        (sk_hbm, sk),
        (sseg_hbm, sseg),
        (x_hbm, xs.at[pl.ds(0, rows)]),
        (up_hbm, up_ref),
        (goal_hbm, goal),
    ]
    loads = [pltpu.make_async_copy(a, b, s_loc.at[i]) for i, (a, b) in enumerate(local)]
    for load in loads:
        load.start()
    loads[0].wait()
    for side in range(2):
        dbuf[2 * f + side] = down_t[:, side * half:(side + 1) * half].astype(BF16)
    pl.semaphore_wait(barrier, N + 1)

    line = [(d, s, z - s * d) for d in range(1, DEPTH) for s in (1, -1)]

    def inside(zp):
        return jnp.logical_and(zp >= 0, zp < DEPTH)

    def piece_send(buf, s_sem, r_sem, kind, i, pred=True):
        send(kind, buf.at[i], buf.at[i], s_sem.at[kind, i], r_sem.at[i], pred)

    def pieces_own(buf, s_sem, r_sem):
        for kind in (UP, DOWN, SIDE):
            piece_send(buf, s_sem, r_sem, kind, 2 * f + c)

    def pieces_line(buf, s_sem, r_sem, d):
        for dd, s, zp in line:
            if dd == d:
                ok, i = inside(zp), 2 * (2 * zp + x) + c
                arrived(buf.at[i], r_sem.at[i], ok)
                for kind in (UP if s > 0 else DOWN, SIDE, CORE):
                    piece_send(buf, s_sem, r_sem, kind, i, ok)

    def pieces_side(buf, s_sem, r_sem, d):
        for dd, s, zp in [(0, 1, z)] + line:
            if dd == d:
                ok, i = (True if d == 0 else inside(zp)), 2 * (2 * zp + other_x) + c
                arrived(buf.at[i], r_sem.at[i], ok)
                piece_send(buf, s_sem, r_sem, CORE, i, ok)

    def pieces_core(buf, r_sem):
        for peer in peers():
            i = 2 * peer + other_c
            arrived(buf.at[i], r_sem.at[i])

    mine, theirs = 2 * c + t, 2 * c + other_t

    def w_send(h, kind, i, pred=True):
        send(kind, wbuf.at[h, i], wbuf.at[h, i], s_w.at[h, kind, i], r_w.at[h, i], pred)

    def w_wait(h, i, pred=True):
        arrived(wbuf.at[h, i], r_w.at[h, i], pred)

    def w_core(h, shard, pred=True):
        pair = wbuf.at[h, pl.ds(4 * shard + 2 * c, 2)]
        send(CORE, pair, pair, s_wc.at[h, shard], r_wc.at[h, shard], pred)

    def w_own(h):
        for kind, q in ((UP, mine), (DOWN, mine), (SIDE, mine), (SIDE, theirs)):
            i = 4 * f + q
            w_send(h, kind, i)

    def w_line(h, d):
        for dd, s, zp in line:
            if dd == d:
                ok, i = inside(zp), 4 * (2 * zp + x) + mine
                w_wait(h, i, ok)
                for kind in (UP if s > 0 else DOWN, SIDE, TWIN):
                    w_send(h, kind, i, ok)

    def w_side(h, d):
        if d == 0:
            i = 4 * (2 * z + other_x) + mine
            w_wait(h, i)
            i = 4 * (2 * z + other_x) + theirs
            w_wait(h, i)
            for kind in (UP, DOWN):
                w_send(h, kind, i)
            w_core(h, 2 * z + other_x)
            return
        for dd, s, zp in line:
            if dd == d:
                ok, i = inside(zp), 4 * (2 * zp + other_x) + mine
                w_wait(h, i, ok)
                if d > 1:
                    w_send(h, TWIN, i, ok)

    def w_twin(h, d, xx):
        for dd, s, zp in line:
            if dd == d:
                ok, i = inside(zp), 4 * (2 * zp + xx) + theirs
                w_wait(h, i, ok)
                w_core(h, 2 * zp + xx, ok)

    def shards(d):
        if d == 0:
            return [(True, f), (True, 2 * z + other_x)]
        return [(inside(zp), 2 * zp + xx) for dd, s, zp in line if dd == d for xx in (x, other_x)]

    def run(pred, step):
        if pred is True:
            step()
        else:
            pl.when(pred)(step)

    def add_base(h, d):
        for n, (ok, shard) in enumerate(shards(d)):
            def step(n=n, shard=shard):
                if d or n:
                    arrived(wbuf.at[h, pl.ds(4 * shard + 2 * other_c, 2)], r_wc.at[h, shard])
                weight = wbuf[h, pl.ds(4 * shard, 4)].reshape(part, wcols)
                both = xs[pl.ds(0, rows + BLOCK), lanes(shard * part, part)]
                base[:, h * wcols:(h + 1) * wcols] += dot(both, weight)

            run(ok, step)

    def train_probs(step):
        b, pair = step // 2, step % 2
        first = max(b - 1, 0) * BLOCK
        position_q = b * BLOCK + lax.broadcasted_iota(jnp.int32, (BLOCK, WINDOW), 0)
        position_k = first + lax.broadcasted_iota(jnp.int32, (BLOCK, WINDOW), 1)
        same = seg_col[pl.ds(b * BLOCK, BLOCK), :] == seg[...].astype(F32)[:, first:first + WINDOW]
        allowed = (position_k <= position_q) & same

        def head_group(g, _):
            q = stack_heads(qs, pl.ds(b * BLOCK, BLOCK), g)
            k = ks[pl.ds(first, WINDOW), lanes(g * HEAD_DIM, HEAD_DIM)]
            probs[b * KV_HEADS + g] = softmax_rows(nt_dot(q, k), allowed)
            return 0

        lax.fori_loop(pair * KV_HEADS // 2, (pair + 1) * KV_HEADS // 2, head_group, 0)

    def score_probs():
        order_q = lax.broadcasted_iota(jnp.int32, (BLOCK, BLOCK), 0)
        order_k = lax.broadcasted_iota(jnp.int32, (BLOCK, BLOCK), 1)
        ids = sseg[...].astype(F32)
        column = jnp.broadcast_to(jnp.concatenate([ids, ids], axis=1), (WINDOW, WINDOW)).T
        allowed = (order_k <= order_q) & (column[:BLOCK, :BLOCK] == ids)

        def head_group(g, _):
            q = stack_heads(sq, pl.ds(0, BLOCK), g)
            sprobs[g] = softmax_rows(nt_dot(q, sk[:, lanes(g * HEAD_DIM, HEAD_DIM)]), allowed)
            return 0

        lax.fori_loop(0, KV_HEADS, head_group, 0)

    def low_step(i, acc):
        return acc + nt_dot(xs[pl.ds(0, rows), lanes(i * half, half)], dbuf[i])

    def attention(h):
        halves = pl.ds(h * wcols, wcols)
        up_half = up_ref[:, halves].astype(BF16)
        mixed = adapter_scale_factor * dot(low_s[...], up_half)
        vals[:, halves] = (base[pl.ds(0, rows), halves] + mixed).astype(BF16)
        for b in range(rows // BLOCK):
            first = max(b - 1, 0) * BLOCK

            def head_group(g, _, b=b, first=first):
                p = probs[b * KV_HEADS + g]
                cols = lanes(g * HEAD_DIM, HEAD_DIM)
                attended = dot(p, vals[pl.ds(first, WINDOW), cols])
                d_out = (attended - stack_heads(goal, pl.ds(b * BLOCK, BLOCK), g).astype(F32)).astype(BF16)
                dvals[pl.ds(first, WINDOW), cols] += tn_dot(p, d_out)
                return 0

            lax.fori_loop(h * KV_HEADS // 2, (h + 1) * KV_HEADS // 2, head_group, 0)

    sx_other = xs.at[pl.ds(rows + BLOCK, BLOCK)]
    dset = (dbuf, s_d, r_d)
    pieces_own(*dset)
    loads[1].wait()
    w_own(0)
    base[...] = jnp.zeros_like(base)
    dvals[...] = jnp.zeros_like(dvals)
    for i in range(3, 6):
        loads[i].wait()
    seg_col[...] = jnp.broadcast_to(seg[...].astype(F32), (WINDOW, rows)).T
    train_probs(0)
    pieces_line(*dset, 1)
    w_line(0, 1)
    w_side(0, 0)
    loads[2].wait()
    w_own(1)
    pieces_side(*dset, 0)
    loads[6].wait()
    send(CORE, xs.at[pl.ds(rows, BLOCK)], sx_other, s_sx, r_sx)
    train_probs(1)
    pieces_line(*dset, 2)
    w_line(0, 2)
    train_probs(2)
    w_side(0, 1)
    pieces_side(*dset, 1)
    w_twin(0, 1, x)
    pieces_line(*dset, 3)
    w_line(0, 3)
    train_probs(3)
    w_line(1, 1)
    w_side(1, 0)
    w_twin(0, 1, other_x)
    pieces_side(*dset, 2)
    train_probs(4)
    w_side(0, 2)
    w_twin(0, 2, x)
    w_line(1, 2)
    train_probs(5)
    pieces_side(*dset, 3)
    w_side(0, 3)
    w_twin(0, 3, x)
    train_probs(6)
    w_side(1, 1)
    w_line(1, 3)
    w_twin(0, 2, other_x)
    train_probs(7)
    w_twin(1, 1, x)
    w_twin(1, 1, other_x)
    for i in range(7, len(loads)):
        loads[i].wait()
    score_probs()
    w_twin(0, 3, other_x)
    pieces_core(dbuf, r_d)
    low = lax.fori_loop(0, 2 * N, low_step, jnp.zeros((rows, low_s.shape[1]), F32)).astype(BF16)
    low_s[...] = low
    w_side(1, 2)
    w_twin(1, 2, x)
    for d in range(DEPTH):
        add_base(0, d)
    w_side(1, 3)
    w_twin(1, 2, other_x)
    w_twin(1, 3, x)
    attention(0)
    w_twin(1, 3, other_x)
    for d in range(DEPTH):
        add_base(1, d)
    attention(1)
    up_half = up_ref[...].astype(BF16)
    dv = dvals[...].astype(BF16)
    dlow_t = (adapter_scale_factor * nt_dot(up_half, dv)).astype(BF16)

    def grad_of(peer, side):
        return dot(dlow_t, xs[pl.ds(0, rows), lanes(peer * part + side * half, half)])

    turns = [lax.rem(z + k, DEPTH) for k in range(1, DEPTH)] + [z]
    order = [2 * zt + xx for zt in turns for xx in (other_x, x)]
    for n, peer in enumerate(order):
        gsend[n] = grad_of(peer, other_c).astype(BF16)
        send(CORE, gsend.at[n], gpair.at[n], s_gp.at[n], r_gp.at[n])
    gu[...] = adapter_scale_factor * tn_dot(low_s[...], dv)
    ucols = VALUE_WIDTH // 2
    send(CORE, gu.at[:, lanes(other_c * ucols, ucols)], gupair, s_up, r_up)

    def core_sum(n):
        mine_of = grad_of(order[n], c)
        arrived(gpair.at[n], r_gp.at[n])
        return mine_of + gpair[n].astype(F32)

    for k in range(DEPTH):
        rsend[k] = core_sum(2 * k).astype(BF16)
        send(SIDE, rsend.at[k], rside.at[k], s_rx.at[k], r_rx.at[k])
    arrived(gupair, r_up)
    gusum[...] = gu[:, lanes(c * ucols, ucols)] + gupair[...]
    send(SIDE, gusum, guside, s_ur, r_ur)
    for k in range(DEPTH):
        total = core_sum(2 * k + 1)
        arrived(rside.at[k], r_rx.at[k])
        total = total + rside[k].astype(F32)
        if k < DEPTH - 1:
            rline[k] = total.astype(BF16)
            peer_send(2 * turns[k] + x, rline.at[k], rrecv.at[k], s_rs.at[k], r_rs.at[k])
    arrived(guside, r_ur)
    guline[z] = (gusum[...] + guside[...]).astype(BF16)
    flush()
    for k in range(DEPTH - 1):
        arrived(rrecv.at[k], r_rs.at[k])
        total = total + rrecv[k].astype(F32)
    new_half = down_t[:, lanes(c * half, half)] - rate_down * total
    ndbuf[f] = new_half.astype(BF16)
    for k in range(DEPTH - 1):
        peer_send(2 * turns[k] + x, ndbuf.at[f], ndbuf.at[f], s_nd.at[k], r_nd.at[f])
    send(SIDE, ndbuf.at[f], ndbuf.at[f], s_nd.at[DEPTH - 1], r_nd.at[f])
    for k in range(DEPTH - 1):
        peer_send(2 * turns[k] + x, guline.at[z], guline.at[z], s_ua.at[k], r_ua.at[z])
    fhalf[...] = new_half
    send(CORE, fhalf, frecv, s_f, r_f)

    def slow_of(shard):
        cols = lanes(shard * part + c * half, half)
        return nt_dot(xs[pl.ds(rows, 2 * BLOCK), cols], ndbuf[shard])

    arrived(sx_other, r_sx)
    slow = slow_of(f)
    for k in range(DEPTH - 1):
        shard = 2 * turns[k] + x
        arrived(ndbuf.at[shard], r_nd.at[shard])
        send(SIDE, ndbuf.at[shard], ndbuf.at[shard], s_nd.at[DEPTH + k], r_nd.at[shard])
    for k in range(DEPTH - 1):
        slow = slow + slow_of(2 * turns[k] + x)
        arrived(guline.at[turns[k]], r_ua.at[turns[k]])
    utotal = guline[0].astype(F32)
    for k in range(1, DEPTH):
        utotal = utotal + guline[k].astype(F32)
    guall[c] = utotal
    send(CORE, guall.at[c], guall.at[c], s_uc, r_uc)
    arrived(frecv, r_f)
    new_down_t[:, lanes(c * half, half)] = fhalf[...]
    new_down_t[:, lanes(other_c * half, half)] = frecv[...]
    for zt in [z] + turns[:-1]:
        shard = 2 * zt + other_x
        arrived(ndbuf.at[shard], r_nd.at[shard])
        slow = slow + slow_of(shard)
    slow_s[...] = slow
    send(CORE, slow_s.at[pl.ds(BLOCK, BLOCK)], slow_recv, s_sl, r_sl)
    arrived(guall.at[other_c], r_uc)
    for side in range(2):
        cols = pl.ds(side * ucols, ucols)
        new_up[:, cols] = up_ref[:, cols] - rate_up * guall[side]
    arrived(slow_recv, r_sl)
    slow = (slow_s[pl.ds(0, BLOCK), :] + slow_recv[...]).astype(BF16)
    svals = (
        base[pl.ds(rows, BLOCK), :] + adapter_scale_factor * dot(slow, new_up[...].astype(BF16))
    ).astype(BF16)
    for g in range(KV_HEADS):
        attended = dot(sprobs[g], svals[:, g * HEAD_DIM:(g + 1) * HEAD_DIM]).astype(BF16)
        for j in range(GROUP):
            at = (g * GROUP + j) * HEAD_DIM
            scored[:, at:at + HEAD_DIM] = attended[j * BLOCK:(j + 1) * BLOCK]

    flush()


def hand_over(a, b, c, a_out, b_out, c_out, a_here, b_here, c_here, s_in, s_out):
    here = (a_here, b_here, c_here)
    loads = [pltpu.make_async_copy(src, dst, s_in.at[i]) for i, (src, dst) in enumerate(zip((a, b, c), here))]
    stores = [
        pltpu.make_async_copy(src, dst, s_out.at[i]) for i, (src, dst) in enumerate(zip(here, (a_out, b_out, c_out)))
    ]
    for load in loads:
        load.start()
    for load, store in zip(loads, stores):
        load.wait()
        store.start()
    for store in stores:
        store.wait()


def fused_body(
    train_input, train_query, train_keys, train_target, train_segments, value_weight, adapter_down, adapter_up,
    score_input, score_query, score_keys, score_segments,
):
    rows, width = train_input.shape[1:]
    part, rank = adapter_down.shape
    half = part // 2
    heads = train_query.shape[2]
    srows = score_input.shape[1]
    vw = value_weight.shape[1]
    hbm, vmem = pl.BlockSpec(memory_space=pltpu.HBM), pl.BlockSpec(memory_space=pltpu.VMEM)
    sem = pltpu.SemaphoreType.DMA
    uc = vw // 2
    piece = (rank, half)
    scratch = [
        pltpu.VMEM((rows + 2 * srows, width), BF16),
        pltpu.VMEM((rows, heads), BF16),
        pltpu.VMEM((rows, vw), BF16),
        pltpu.VMEM((rows, heads), BF16),
        pltpu.VMEM((1, rows), jnp.int32),
        pltpu.VMEM((rank, part), F32),
        pltpu.VMEM((rank, vw), F32),
        pltpu.VMEM((srows, heads), BF16),
        pltpu.VMEM((srows, vw), BF16),
        pltpu.VMEM((1, srows), jnp.int32),
        pltpu.VMEM((rows, WINDOW), F32),
        pltpu.VMEM((2, 4 * N, part // 4, vw // 2), BF16),
        pltpu.VMEM((2 * N, *piece), BF16),
        pltpu.VMEM((N, *piece), BF16),
        pltpu.VMEM((rows // BLOCK * KV_HEADS, GROUP * BLOCK, WINDOW), BF16),
        pltpu.VMEM((KV_HEADS, GROUP * BLOCK, BLOCK), BF16),
        pltpu.VMEM((rows + srows, vw), F32),
        pltpu.VMEM((rows, vw), BF16),
        pltpu.VMEM((rows, vw), F32),
        pltpu.VMEM((rows, rank), BF16),
        pltpu.VMEM((2 * srows, rank), F32),
        pltpu.VMEM((srows, rank), F32),
        pltpu.VMEM((N, *piece), BF16),
        pltpu.VMEM((N, *piece), BF16),
        pltpu.VMEM((DEPTH, *piece), BF16),
        pltpu.VMEM((DEPTH, *piece), BF16),
        pltpu.VMEM((DEPTH - 1, *piece), BF16),
        pltpu.VMEM((DEPTH - 1, *piece), BF16),
        pltpu.VMEM(piece, F32),
        pltpu.VMEM(piece, F32),
        pltpu.VMEM((rank, vw), F32),
        pltpu.VMEM((rank, uc), F32),
        pltpu.VMEM((rank, uc), F32),
        pltpu.VMEM((rank, uc), F32),
        pltpu.VMEM((DEPTH, rank, uc), BF16),
        pltpu.VMEM((2, rank, uc), F32),
        sem((13,)),
        sem((2, 5, 4 * N)), sem((2, 4 * N)),
        sem((2, N)), sem((2, N)),
        sem((5, 2 * N)), sem((2 * N,)),
        sem((2 * DEPTH - 1,)), sem((N,)),
        sem((N,)), sem((N,)),
        sem((DEPTH,)), sem((DEPTH,)),
        sem((DEPTH - 1,)), sem((DEPTH - 1,)),
        sem, sem,
        sem, sem,
        sem, sem,
        sem((DEPTH - 1,)), sem((DEPTH,)),
        sem, sem,
        sem, sem,
        sem, sem,
    ]
    new_down_t, new_up, scored = pl.pallas_call(
        fused_kernel,
        out_shape=(
            jax.ShapeDtypeStruct((rank, part), F32),
            jax.ShapeDtypeStruct(adapter_up.shape, F32),
            jax.ShapeDtypeStruct((srows, heads), BF16),
        ),
        in_specs=[hbm] * 12,
        out_specs=(vmem, vmem, vmem),
        scratch_shapes=scratch,
        compiler_params=pltpu.CompilerParams(
            collective_id=0, has_side_effects=True, vmem_limit_bytes=56 * 1024 * 1024
        ),
        name="test_time_step",
    )(
        train_input[0], train_query[0], train_keys[0], train_target[0], train_segments.reshape(1, rows),
        value_weight.reshape(4, part // 4, vw), adapter_down.T, adapter_up,
        score_input[0], score_query[0], score_keys[0], score_segments.reshape(1, srows),
    )
    results = (new_down_t, new_up, scored)
    shapes = [(a.shape, a.dtype) for a in results]
    new_down_t, new_up, scored = pl.pallas_call(
        hand_over,
        out_shape=tuple(jax.ShapeDtypeStruct(*a) for a in shapes),
        in_specs=[hbm] * 3,
        out_specs=(hbm,) * 3,
        scratch_shapes=[*(pltpu.VMEM(*a) for a in shapes), sem((3,)), sem((3,))],
        compiler_params=pltpu.CompilerParams(vmem_limit_bytes=56 * 1024 * 1024),
        name="hand_over",
    )(*results)
    return (new_down_t.T, new_up, scored[None])


def solution(mesh):
    in_specs = (
        P(("task", "view"), "fsdp", None),
        P(("task", "view"), "fsdp", None),
        P(("task", "view"), "fsdp", None),
        P(("task", "view"), "fsdp", None),
        P(("task", "view"), "fsdp", None),
        P("fsdp", None),
        P(("task", "fsdp"), None),
        P("task", None),
        P(("task", "view"), "fsdp", None),
        P(("task", "view"), "fsdp", None),
        P(("task", "view"), "fsdp", None),
        P(("task", "view"), "fsdp", None),
    )
    out_specs = (P(("task", "fsdp"), None), P("task", None), P(("task", "view"), "fsdp", None))
    local = fused_body if (mesh.shape["fsdp"], mesh.shape["view"]) == (8, 2) else body
    return jax.shard_map(local, mesh=mesh, in_specs=in_specs, out_specs=out_specs, check_vma=False)
```

```python
import jax
import jax.numpy as jnp
from jax import lax
from jax.experimental import pallas as pl
from jax.experimental.pallas import tpu as pltpu
from jax.sharding import PartitionSpec as P

Q_HEADS = 32
KV_HEADS = 4
HEAD_DIM = 128
GROUP = 8
VALUE_WIDTH = 512


adapter_scale_factor = 0.5
rate_down = 2e-05
rate_up = 0.001


def attend_row(query, keyset, value_rows, segment):
    length = query.shape[0]
    query_heads = query.reshape(length, KV_HEADS, GROUP, HEAD_DIM)
    key_heads = keyset.reshape(length, KV_HEADS, HEAD_DIM)
    logits = jnp.einsum(
        "qgjd,kgd->gjqk", query_heads, key_heads, preferred_element_type=jnp.float32
    ) * HEAD_DIM ** (-0.5)
    positions = jnp.arange(length, dtype=jnp.int32)
    allowed = (positions[None, :] <= positions[:, None]) & (segment[:, None] == segment[None, :])
    logits = jnp.where(allowed, logits, -1e30)
    peak = jnp.max(logits, axis=-1, keepdims=True)
    weights = jnp.exp(logits - peak)
    probs = (weights / jnp.sum(weights, axis=-1, keepdims=True)).astype(jnp.bfloat16)
    value_heads = value_rows.reshape(length, KV_HEADS, HEAD_DIM)
    attended = jnp.einsum("gjqk,kgd->qgjd", probs, value_heads, preferred_element_type=jnp.float32)
    return (probs, attended.reshape(length, Q_HEADS * HEAD_DIM))


def values_grad(probs, d_out):
    length = d_out.shape[0]
    heads = d_out.reshape(length, KV_HEADS, GROUP, HEAD_DIM)
    summed = jnp.einsum("gjqk,qgjd->kgd", probs, heads, preferred_element_type=jnp.float32)
    return summed.reshape(length, VALUE_WIDTH).astype(jnp.bfloat16)


def add_pieces(rows_in, pieces):
    return (
        jnp.dot(rows_in, pieces[0], preferred_element_type=jnp.float32),
        jnp.dot(rows_in, pieces[1], preferred_element_type=jnp.float32),
    )


def body(
    train_input,
    train_query,
    train_keys,
    train_target,
    train_segments,
    value_weight,
    adapter_down,
    adapter_up,
    score_input,
    score_query,
    score_keys,
    score_segments,
):
    width = train_input.shape[-1]
    value_width = value_weight.shape[1]
    count_rows = train_segments.shape[0] * train_segments.shape[1]
    row_length = train_segments.shape[2]
    score_length = score_segments.shape[2]
    down_half = adapter_down.astype(jnp.bfloat16)
    upper_weight_half = adapter_up.astype(jnp.bfloat16)
    train_rows = train_input.reshape(-1, width)
    frozen_base_weight, low = add_pieces(
        train_rows,
        (
            lax.all_gather(value_weight, "fsdp", axis=0, tiled=True),
            lax.all_gather(down_half, "fsdp", axis=0, tiled=True),
        ),
    )
    lower_rank_half = low.astype(jnp.bfloat16)
    value_rows = (
        frozen_base_weight
        + adapter_scale_factor
        * jnp.dot(lower_rank_half, upper_weight_half, preferred_element_type=jnp.float32)
    ).astype(jnp.bfloat16)
    probs, attended = jax.vmap(attend_row)(
        train_query,
        train_keys,
        value_rows.reshape(count_rows, row_length, -1),
        train_segments.reshape(count_rows, row_length),
    )
    d_out = (attended - train_target.astype(jnp.float32)).astype(jnp.bfloat16)
    value_output_gradient = jax.vmap(values_grad)(probs, d_out).reshape(-1, value_width)
    low_rank_gradient = (
        adapter_scale_factor
        * lax.dot_general(
            value_output_gradient,
            upper_weight_half,
            (((1,), (1,)), ((), ())),
            preferred_element_type=jnp.float32,
        )
    ).astype(jnp.bfloat16)
    local_up_gradient = adapter_scale_factor * lax.dot_general(
        lower_rank_half,
        value_output_gradient,
        (((0,), (0,)), ((), ())),
        preferred_element_type=jnp.float32,
    )
    grad_down = lax.psum_scatter(
        lax.dot_general(
            train_rows,
            low_rank_gradient,
            (((0,), (0,)), ((), ())),
            preferred_element_type=jnp.float32,
        ),
        "fsdp",
        scatter_dimension=0,
        tiled=True,
    )
    grad_down = lax.psum(grad_down, "view")
    up_weight_gradient = lax.psum(local_up_gradient, ("fsdp", "view"))
    new_down = adapter_down - rate_down * grad_down
    new_up = adapter_up - rate_up * up_weight_gradient
    new_down_half = new_down.astype(jnp.bfloat16)
    new_up_half = new_up.astype(jnp.bfloat16)
    score_rows = score_input.reshape(-1, width)
    score_base, score_low = add_pieces(
        score_rows,
        (
            lax.all_gather(value_weight, "fsdp", axis=0, tiled=True),
            lax.all_gather(new_down_half, "fsdp", axis=0, tiled=True),
        ),
    )
    score_values = (
        score_base
        + adapter_scale_factor
        * jnp.dot(score_low.astype(jnp.bfloat16), new_up_half, preferred_element_type=jnp.float32)
    ).astype(jnp.bfloat16)
    score_probs, score_attended = jax.vmap(attend_row)(
        score_query,
        score_keys,
        score_values.reshape(count_rows, score_length, -1),
        score_segments.reshape(count_rows, score_length),
    )
    scored = score_attended.astype(jnp.bfloat16)
    return (new_down, new_up, scored)


F32, BF16 = jnp.float32, jnp.bfloat16
N, DEPTH = 8, 4
BLOCK = 64
WINDOW = 2 * BLOCK
NT = (((1,), (1,)), ((), ()))
TN = (((0,), (0,)), ((), ()))
UP, DOWN, SIDE, TWIN, CORE = range(5)


def nt_dot(a, b):
    return lax.dot_general(a, b, NT, preferred_element_type=F32)


def tn_dot(a, b):
    return lax.dot_general(a, b, TN, preferred_element_type=F32)


def dot(a, b):
    return jnp.dot(a, b, preferred_element_type=F32)


def lanes(start, size):
    return pl.ds(pl.multiple_of(start, size), size)


def stack_heads(ref, rows, g):
    return jnp.concatenate(
        [ref[rows, lanes((g * GROUP + j) * HEAD_DIM, HEAD_DIM)] for j in range(GROUP)], axis=0
    )


def softmax_rows(logits, allowed):
    shape = logits.shape
    logits = (logits * HEAD_DIM ** (-0.5)).reshape(GROUP, BLOCK, shape[-1])
    logits = jnp.where(allowed[None], logits, -1e30)
    weights = jnp.exp(logits - jnp.max(logits, axis=-1, keepdims=True))
    probs = weights * (1.0 / jnp.sum(weights, axis=-1, keepdims=True))
    return probs.reshape(shape).astype(BF16)


def fused_kernel(
    x_hbm, q_hbm, k_hbm, goal_hbm, seg_hbm, w_hbm, down_hbm, up_hbm, sx_hbm, sq_hbm, sk_hbm, sseg_hbm,
    new_down_t, new_up, scored,
    xs, qs, ks, goal, seg, down_t, up_ref, sq, sk, sseg, seg_col, wbuf, dbuf, ndbuf, probs, sprobs, base, vals, dvals,
    low_s, slow_s, slow_recv, gsend, gpair, rsend, rside, rline, rrecv, fhalf, frecv,
    gu, gupair, gusum, guside, guline, guall,
    s_loc, s_w, r_w, s_wc, r_wc, s_d, r_d, s_nd, r_nd, s_gp, r_gp, s_rx, r_rx, s_rs, r_rs, s_f, r_f,
    s_up, r_up, s_ur, r_ur, s_ua, r_ua, s_uc, r_uc, s_sx, r_sx, s_sl, r_sl,
):
    t, f, c = lax.axis_index("task"), lax.axis_index("fsdp"), lax.axis_index("view")
    z, x = lax.div(f, 2), lax.rem(f, 2)
    other_t, other_x, other_c = 1 - t, 1 - x, 1 - c
    width = xs.shape[1]
    part = width // N
    half = part // 2
    rows = vals.shape[0]
    late = []
    wcols = VALUE_WIDTH // 2

    def device(kind):
        return {
            UP: {"fsdp": f + 2},
            DOWN: {"fsdp": f - 2},
            SIDE: {"fsdp": 2 * z + other_x},
            TWIN: {"task": other_t},
            CORE: {"view": other_c},
        }[kind]

    def exists(kind):
        return {UP: z < DEPTH - 1, DOWN: z > 0}.get(kind, True)

    def start(make, pred=True):
        if pred is True:
            make().start()
        else:
            pl.when(pred)(lambda: make().start())
        late.append((make, pred))

    def send(kind, src, dst, s_sem, r_sem, pred=True):
        where = exists(kind)
        if where is not True:
            pred = where if pred is True else jnp.logical_and(where, pred)

        def make():
            return pltpu.make_async_remote_copy(
                src_ref=src, dst_ref=dst, send_sem=s_sem, recv_sem=r_sem,
                device_id=device(kind), device_id_type=pl.DeviceIdType.MESH,
            )

        start(make, pred)

    def peer_send(peer, src, dst, s_sem, r_sem):
        def make():
            return pltpu.make_async_remote_copy(
                src_ref=src, dst_ref=dst, send_sem=s_sem, recv_sem=r_sem,
                device_id={"fsdp": peer}, device_id_type=pl.DeviceIdType.MESH,
            )

        start(make)

    def arrived(dst, r_sem, pred=True):
        def wait():
            pltpu.make_async_remote_copy(
                src_ref=dst, dst_ref=dst, send_sem=r_sem, recv_sem=r_sem,
                device_id={"view": other_c}, device_id_type=pl.DeviceIdType.MESH,
            ).wait_recv()

        if pred is True:
            wait()
        else:
            pl.when(pred)(wait)

    def flush(count):
        def finish(make):
            make().wait_send()

        for make, pred in late[:count]:
            if pred is True:
                finish(make)
            else:
                pl.when(pred)(lambda make=make: finish(make))
        del late[:count]

    def peers():
        return [lax.rem(f + k, N) for k in range(1, N)]

    barrier = pltpu.get_barrier_semaphore()
    for peer in peers():
        pl.semaphore_signal(barrier, inc=1, device_id={"fsdp": peer}, device_id_type=pl.DeviceIdType.MESH)
    for kind in (TWIN, CORE):
        pl.semaphore_signal(barrier, inc=1, device_id=device(kind), device_id_type=pl.DeviceIdType.MESH)

    local = [(down_hbm, down_t)]
    local += [(w_hbm.at[:, :, pl.ds(h * wcols, wcols)], wbuf.at[h, pl.ds(4 * f, 4)]) for h in range(2)]
    local += [
        (q_hbm, qs),
        (k_hbm, ks),
        (seg_hbm, seg),
        (sx_hbm, xs.at[pl.ds(rows, BLOCK)]),
        (sq_hbm, sq),
        (sk_hbm, sk),
        (sseg_hbm, sseg),
        (x_hbm, xs.at[pl.ds(0, rows)]),
        (up_hbm, up_ref),
        (goal_hbm, goal),
    ]
    loads = [pltpu.make_async_copy(a, b, s_loc.at[i]) for i, (a, b) in enumerate(local)]
    for load in loads:
        load.start()
    loads[0].wait()
    for side in range(2):
        dbuf[2 * f + side] = down_t[:, side * half:(side + 1) * half].astype(BF16)
    pl.semaphore_wait(barrier, N + 1)

    line = [(d, s, z - s * d) for d in range(1, DEPTH) for s in (1, -1)]

    def inside(zp):
        return jnp.logical_and(zp >= 0, zp < DEPTH)

    def piece_send(buf, s_sem, r_sem, kind, i, pred=True):
        send(kind, buf.at[i], buf.at[i], s_sem.at[kind, i], r_sem.at[i], pred)

    def pieces_own(buf, s_sem, r_sem):
        for kind in (UP, DOWN, SIDE):
            piece_send(buf, s_sem, r_sem, kind, 2 * f + c)

    def pieces_line(buf, s_sem, r_sem, d):
        for dd, s, zp in line:
            if dd == d:
                ok, i = inside(zp), 2 * (2 * zp + x) + c
                arrived(buf.at[i], r_sem.at[i], ok)
                for kind in (UP if s > 0 else DOWN, SIDE, CORE):
                    piece_send(buf, s_sem, r_sem, kind, i, ok)

    def pieces_side(buf, s_sem, r_sem, d):
        for dd, s, zp in [(0, 1, z)] + line:
            if dd == d:
                ok, i = (True if d == 0 else inside(zp)), 2 * (2 * zp + other_x) + c
                arrived(buf.at[i], r_sem.at[i], ok)
                piece_send(buf, s_sem, r_sem, CORE, i, ok)

    def pieces_core(buf, r_sem):
        for peer in peers():
            i = 2 * peer + other_c
            arrived(buf.at[i], r_sem.at[i])

    mine, theirs = 2 * c + t, 2 * c + other_t

    def w_send(h, kind, i, pred=True):
        send(kind, wbuf.at[h, i], wbuf.at[h, i], s_w.at[h, kind, i], r_w.at[h, i], pred)

    def w_wait(h, i, pred=True):
        arrived(wbuf.at[h, i], r_w.at[h, i], pred)

    def w_core(h, shard, pred=True):
        pair = wbuf.at[h, pl.ds(4 * shard + 2 * c, 2)]
        send(CORE, pair, pair, s_wc.at[h, shard], r_wc.at[h, shard], pred)

    def w_own(h):
        for kind, q in ((UP, mine), (DOWN, mine), (SIDE, mine), (SIDE, theirs)):
            i = 4 * f + q
            w_send(h, kind, i)

    def w_line(h, d):
        for dd, s, zp in line:
            if dd == d:
                ok, i = inside(zp), 4 * (2 * zp + x) + mine
                w_wait(h, i, ok)
                for kind in (UP if s > 0 else DOWN, SIDE, TWIN):
                    w_send(h, kind, i, ok)

    def w_side(h, d):
        if d == 0:
            i = 4 * (2 * z + other_x) + mine
            w_wait(h, i)
            i = 4 * (2 * z + other_x) + theirs
            w_wait(h, i)
            for kind in (UP, DOWN):
                w_send(h, kind, i)
            w_core(h, 2 * z + other_x)
            return
        for dd, s, zp in line:
            if dd == d:
                ok, i = inside(zp), 4 * (2 * zp + other_x) + mine
                w_wait(h, i, ok)
                if d > 1:
                    w_send(h, TWIN, i, ok)

    def w_twin(h, d, xx):
        for dd, s, zp in line:
            if dd == d:
                ok, i = inside(zp), 4 * (2 * zp + xx) + theirs
                w_wait(h, i, ok)
                w_core(h, 2 * zp + xx, ok)

    def shards(d):
        if d == 0:
            return [(True, f), (True, 2 * z + other_x)]
        return [(inside(zp), 2 * zp + xx) for dd, s, zp in line if dd == d for xx in (x, other_x)]

    def run(pred, step):
        if pred is True:
            step()
        else:
            pl.when(pred)(step)

    def add_base(h, d):
        for n, (ok, shard) in enumerate(shards(d)):
            def step(n=n, shard=shard):
                if d or n:
                    arrived(wbuf.at[h, pl.ds(4 * shard + 2 * other_c, 2)], r_wc.at[h, shard])
                weight = wbuf[h, pl.ds(4 * shard, 4)].reshape(part, wcols)
                both = xs[pl.ds(0, rows + BLOCK), lanes(shard * part, part)]
                base[:, h * wcols:(h + 1) * wcols] += dot(both, weight)

            run(ok, step)

    def train_probs(step):
        b, pair = step // 2, step % 2
        first = max(b - 1, 0) * BLOCK
        position_q = b * BLOCK + lax.broadcasted_iota(jnp.int32, (BLOCK, WINDOW), 0)
        position_k = first + lax.broadcasted_iota(jnp.int32, (BLOCK, WINDOW), 1)
        same = seg_col[pl.ds(b * BLOCK, BLOCK), :] == seg[...].astype(F32)[:, first:first + WINDOW]
        allowed = (position_k <= position_q) & same

        def head_group(g, _):
            q = stack_heads(qs, pl.ds(b * BLOCK, BLOCK), g)
            k = ks[pl.ds(first, WINDOW), lanes(g * HEAD_DIM, HEAD_DIM)]
            probs[b * KV_HEADS + g] = softmax_rows(nt_dot(q, k), allowed)
            return 0

        lax.fori_loop(pair * KV_HEADS // 2, (pair + 1) * KV_HEADS // 2, head_group, 0)

    def score_probs():
        order_q = lax.broadcasted_iota(jnp.int32, (BLOCK, BLOCK), 0)
        order_k = lax.broadcasted_iota(jnp.int32, (BLOCK, BLOCK), 1)
        ids = sseg[...].astype(F32)
        column = jnp.broadcast_to(jnp.concatenate([ids, ids], axis=1), (WINDOW, WINDOW)).T
        allowed = (order_k <= order_q) & (column[:BLOCK, :BLOCK] == ids)

        def head_group(g, _):
            q = stack_heads(sq, pl.ds(0, BLOCK), g)
            sprobs[g] = softmax_rows(nt_dot(q, sk[:, lanes(g * HEAD_DIM, HEAD_DIM)]), allowed)
            return 0

        lax.fori_loop(0, KV_HEADS, head_group, 0)

    def low_step(i, acc):
        return acc + nt_dot(xs[pl.ds(0, rows), lanes(i * half, half)], dbuf[i])

    def attention(h):
        halves = pl.ds(h * wcols, wcols)
        up_half = up_ref[:, halves].astype(BF16)
        mixed = adapter_scale_factor * dot(low_s[...], up_half)
        vals[:, halves] = (base[pl.ds(0, rows), halves] + mixed).astype(BF16)
        for b in range(rows // BLOCK):
            first = max(b - 1, 0) * BLOCK

            def head_group(g, _, b=b, first=first):
                p = probs[b * KV_HEADS + g]
                cols = lanes(g * HEAD_DIM, HEAD_DIM)
                attended = dot(p, vals[pl.ds(first, WINDOW), cols])
                d_out = (attended - stack_heads(goal, pl.ds(b * BLOCK, BLOCK), g).astype(F32)).astype(BF16)
                dvals[pl.ds(first, WINDOW), cols] += tn_dot(p, d_out)
                return 0

            lax.fori_loop(h * KV_HEADS // 2, (h + 1) * KV_HEADS // 2, head_group, 0)

    sx_other = xs.at[pl.ds(rows + BLOCK, BLOCK)]
    dset = (dbuf, s_d, r_d)
    pieces_own(*dset)
    loads[1].wait()
    w_own(0)
    base[...] = jnp.zeros_like(base)
    dvals[...] = jnp.zeros_like(dvals)
    for i in range(3, 6):
        loads[i].wait()
    seg_col[...] = jnp.broadcast_to(seg[...].astype(F32), (WINDOW, rows)).T
    train_probs(0)
    pieces_line(*dset, 1)
    w_line(0, 1)
    w_side(0, 0)
    loads[2].wait()
    w_own(1)
    pieces_side(*dset, 0)
    loads[6].wait()
    send(CORE, xs.at[pl.ds(rows, BLOCK)], sx_other, s_sx, r_sx)
    train_probs(1)
    pieces_line(*dset, 2)
    w_line(0, 2)
    train_probs(2)
    w_side(0, 1)
    pieces_side(*dset, 1)
    w_twin(0, 1, x)
    pieces_line(*dset, 3)
    w_line(0, 3)
    train_probs(3)
    w_line(1, 1)
    w_side(1, 0)
    w_twin(0, 1, other_x)
    pieces_side(*dset, 2)
    train_probs(4)
    w_side(0, 2)
    w_twin(0, 2, x)
    w_line(1, 2)
    train_probs(5)
    pieces_side(*dset, 3)
    w_side(0, 3)
    w_twin(0, 3, x)
    train_probs(6)
    w_side(1, 1)
    w_line(1, 3)
    w_twin(0, 2, other_x)
    train_probs(7)
    w_twin(1, 1, x)
    w_twin(1, 1, other_x)
    for i in range(7, len(loads)):
        loads[i].wait()
    score_probs()
    w_twin(0, 3, other_x)
    pieces_core(dbuf, r_d)
    low = lax.fori_loop(0, 2 * N, low_step, jnp.zeros((rows, low_s.shape[1]), F32)).astype(BF16)
    low_s[...] = low
    w_side(1, 2)
    w_twin(1, 2, x)
    for d in range(DEPTH):
        add_base(0, d)
    w_side(1, 3)
    w_twin(1, 2, other_x)
    w_twin(1, 3, x)
    attention(0)
    w_twin(1, 3, other_x)
    for d in range(DEPTH):
        add_base(1, d)
    attention(1)
    up_half = up_ref[...].astype(BF16)
    dv = dvals[...].astype(BF16)
    dlow_t = (adapter_scale_factor * nt_dot(up_half, dv)).astype(BF16)

    def grad_of(peer, side):
        return dot(dlow_t, xs[pl.ds(0, rows), lanes(peer * part + side * half, half)])

    turns = [lax.rem(z + k, DEPTH) for k in range(1, DEPTH)] + [z]
    order = [2 * zt + xx for zt in turns for xx in (other_x, x)]
    older = len(late)

    def to_core(n):
        gsend[n] = grad_of(order[n], other_c).astype(BF16)
        send(CORE, gsend.at[n], gpair.at[n], s_gp.at[n], r_gp.at[n])

    def core_sum(n):
        mine_of = grad_of(order[n], c)
        arrived(gpair.at[n], r_gp.at[n])
        return mine_of + gpair[n].astype(F32)

    for k in range(DEPTH):
        to_core(2 * k)
    for k in range(DEPTH):
        to_core(2 * k + 1)
        rsend[k] = core_sum(2 * k).astype(BF16)
        send(SIDE, rsend.at[k], rside.at[k], s_rx.at[k], r_rx.at[k])
    ucols = VALUE_WIDTH // 2
    gu[...] = adapter_scale_factor * tn_dot(low_s[...], dv)
    send(CORE, gu.at[:, lanes(other_c * ucols, ucols)], gupair, s_up, r_up)
    for k in range(DEPTH):
        total = core_sum(2 * k + 1)
        arrived(rside.at[k], r_rx.at[k])
        total = total + rside[k].astype(F32)
        if k < DEPTH - 1:
            rline[k] = total.astype(BF16)
            peer_send(2 * turns[k] + x, rline.at[k], rrecv.at[k], s_rs.at[k], r_rs.at[k])
    arrived(gupair, r_up)
    gusum[...] = gu[:, lanes(c * ucols, ucols)] + gupair[...]
    send(SIDE, gusum, guside, s_ur, r_ur)
    flush(older)
    for k in range(DEPTH - 1):
        arrived(rrecv.at[k], r_rs.at[k])
        total = total + rrecv[k].astype(F32)
    new_half = down_t[:, lanes(c * half, half)] - rate_down * total
    ndbuf[f] = new_half.astype(BF16)
    for k in range(DEPTH - 1):
        peer_send(2 * turns[k] + x, ndbuf.at[f], ndbuf.at[f], s_nd.at[k], r_nd.at[f])
    send(SIDE, ndbuf.at[f], ndbuf.at[f], s_nd.at[DEPTH - 1], r_nd.at[f])
    arrived(guside, r_ur)
    guline[z] = (gusum[...] + guside[...]).astype(BF16)
    for k in range(DEPTH - 1):
        peer_send(2 * turns[k] + x, guline.at[z], guline.at[z], s_ua.at[k], r_ua.at[z])
    fhalf[...] = new_half
    send(CORE, fhalf, frecv, s_f, r_f)

    def slow_of(shard):
        cols = lanes(shard * part + c * half, half)
        return nt_dot(xs[pl.ds(rows, 2 * BLOCK), cols], ndbuf[shard])

    arrived(sx_other, r_sx)
    slow = slow_of(f)
    for k in range(DEPTH - 1):
        shard = 2 * turns[k] + x
        arrived(ndbuf.at[shard], r_nd.at[shard])
        send(SIDE, ndbuf.at[shard], ndbuf.at[shard], s_nd.at[DEPTH + k], r_nd.at[shard])
    for k in range(DEPTH - 1):
        slow = slow + slow_of(2 * turns[k] + x)
        arrived(guline.at[turns[k]], r_ua.at[turns[k]])
    utotal = guline[0].astype(F32)
    for k in range(1, DEPTH):
        utotal = utotal + guline[k].astype(F32)
    guall[c] = utotal
    send(CORE, guall.at[c], guall.at[c], s_uc, r_uc)
    arrived(frecv, r_f)
    new_down_t[:, lanes(c * half, half)] = fhalf[...]
    new_down_t[:, lanes(other_c * half, half)] = frecv[...]
    for zt in [z] + turns[:-1]:
        shard = 2 * zt + other_x
        arrived(ndbuf.at[shard], r_nd.at[shard])
        slow = slow + slow_of(shard)
    slow_s[...] = slow
    send(CORE, slow_s.at[pl.ds(BLOCK, BLOCK)], slow_recv, s_sl, r_sl)
    arrived(guall.at[other_c], r_uc)
    for side in range(2):
        cols = pl.ds(side * ucols, ucols)
        new_up[:, cols] = up_ref[:, cols] - rate_up * guall[side]
    arrived(slow_recv, r_sl)
    slow = (slow_s[pl.ds(0, BLOCK), :] + slow_recv[...]).astype(BF16)
    svals = (
        base[pl.ds(rows, BLOCK), :] + adapter_scale_factor * dot(slow, new_up[...].astype(BF16))
    ).astype(BF16)
    for g in range(KV_HEADS):
        attended = dot(sprobs[g], svals[:, g * HEAD_DIM:(g + 1) * HEAD_DIM]).astype(BF16)
        for j in range(GROUP):
            at = (g * GROUP + j) * HEAD_DIM
            scored[:, at:at + HEAD_DIM] = attended[j * BLOCK:(j + 1) * BLOCK]

    flush(len(late))


def hand_over(a, b, c, a_out, b_out, c_out, a_here, b_here, c_here, s_in, s_out):
    here = (a_here, b_here, c_here)
    loads = [pltpu.make_async_copy(src, dst, s_in.at[i]) for i, (src, dst) in enumerate(zip((a, b, c), here))]
    stores = [
        pltpu.make_async_copy(src, dst, s_out.at[i]) for i, (src, dst) in enumerate(zip(here, (a_out, b_out, c_out)))
    ]
    for load in loads:
        load.start()
    for load, store in zip(loads, stores):
        load.wait()
        store.start()
    for store in stores:
        store.wait()


def fused_body(
    train_input, train_query, train_keys, train_target, train_segments, value_weight, adapter_down, adapter_up,
    score_input, score_query, score_keys, score_segments,
):
    rows, width = train_input.shape[1:]
    part, rank = adapter_down.shape
    half = part // 2
    heads = train_query.shape[2]
    srows = score_input.shape[1]
    vw = value_weight.shape[1]
    hbm, vmem = pl.BlockSpec(memory_space=pltpu.HBM), pl.BlockSpec(memory_space=pltpu.VMEM)
    sem = pltpu.SemaphoreType.DMA
    uc = vw // 2
    piece = (rank, half)
    scratch = [
        pltpu.VMEM((rows + 2 * srows, width), BF16),
        pltpu.VMEM((rows, heads), BF16),
        pltpu.VMEM((rows, vw), BF16),
        pltpu.VMEM((rows, heads), BF16),
        pltpu.VMEM((1, rows), jnp.int32),
        pltpu.VMEM((rank, part), F32),
        pltpu.VMEM((rank, vw), F32),
        pltpu.VMEM((srows, heads), BF16),
        pltpu.VMEM((srows, vw), BF16),
        pltpu.VMEM((1, srows), jnp.int32),
        pltpu.VMEM((rows, WINDOW), F32),
        pltpu.VMEM((2, 4 * N, part // 4, vw // 2), BF16),
        pltpu.VMEM((2 * N, *piece), BF16),
        pltpu.VMEM((N, *piece), BF16),
        pltpu.VMEM((rows // BLOCK * KV_HEADS, GROUP * BLOCK, WINDOW), BF16),
        pltpu.VMEM((KV_HEADS, GROUP * BLOCK, BLOCK), BF16),
        pltpu.VMEM((rows + srows, vw), F32),
        pltpu.VMEM((rows, vw), BF16),
        pltpu.VMEM((rows, vw), F32),
        pltpu.VMEM((rows, rank), BF16),
        pltpu.VMEM((2 * srows, rank), F32),
        pltpu.VMEM((srows, rank), F32),
        pltpu.VMEM((N, *piece), BF16),
        pltpu.VMEM((N, *piece), BF16),
        pltpu.VMEM((DEPTH, *piece), BF16),
        pltpu.VMEM((DEPTH, *piece), BF16),
        pltpu.VMEM((DEPTH - 1, *piece), BF16),
        pltpu.VMEM((DEPTH - 1, *piece), BF16),
        pltpu.VMEM(piece, F32),
        pltpu.VMEM(piece, F32),
        pltpu.VMEM((rank, vw), F32),
        pltpu.VMEM((rank, uc), F32),
        pltpu.VMEM((rank, uc), F32),
        pltpu.VMEM((rank, uc), F32),
        pltpu.VMEM((DEPTH, rank, uc), BF16),
        pltpu.VMEM((2, rank, uc), F32),
        sem((13,)),
        sem((2, 5, 4 * N)), sem((2, 4 * N)),
        sem((2, N)), sem((2, N)),
        sem((5, 2 * N)), sem((2 * N,)),
        sem((2 * DEPTH - 1,)), sem((N,)),
        sem((N,)), sem((N,)),
        sem((DEPTH,)), sem((DEPTH,)),
        sem((DEPTH - 1,)), sem((DEPTH - 1,)),
        sem, sem,
        sem, sem,
        sem, sem,
        sem((DEPTH - 1,)), sem((DEPTH,)),
        sem, sem,
        sem, sem,
        sem, sem,
    ]
    new_down_t, new_up, scored = pl.pallas_call(
        fused_kernel,
        out_shape=(
            jax.ShapeDtypeStruct((rank, part), F32),
            jax.ShapeDtypeStruct(adapter_up.shape, F32),
            jax.ShapeDtypeStruct((srows, heads), BF16),
        ),
        in_specs=[hbm] * 12,
        out_specs=(vmem, vmem, vmem),
        scratch_shapes=scratch,
        compiler_params=pltpu.CompilerParams(
            collective_id=0, has_side_effects=True, vmem_limit_bytes=56 * 1024 * 1024
        ),
        name="test_time_step",
    )(
        train_input[0], train_query[0], train_keys[0], train_target[0], train_segments.reshape(1, rows),
        value_weight.reshape(4, part // 4, vw), adapter_down.T, adapter_up,
        score_input[0], score_query[0], score_keys[0], score_segments.reshape(1, srows),
    )
    results = (new_down_t, new_up, scored)
    shapes = [(a.shape, a.dtype) for a in results]
    new_down_t, new_up, scored = pl.pallas_call(
        hand_over,
        out_shape=tuple(jax.ShapeDtypeStruct(*a) for a in shapes),
        in_specs=[hbm] * 3,
        out_specs=(hbm,) * 3,
        scratch_shapes=[*(pltpu.VMEM(*a) for a in shapes), sem((3,)), sem((3,))],
        compiler_params=pltpu.CompilerParams(vmem_limit_bytes=56 * 1024 * 1024),
        name="hand_over",
    )(*results)
    return (new_down_t.T, new_up, scored[None])


def solution(mesh):
    in_specs = (
        P(("task", "view"), "fsdp", None),
        P(("task", "view"), "fsdp", None),
        P(("task", "view"), "fsdp", None),
        P(("task", "view"), "fsdp", None),
        P(("task", "view"), "fsdp", None),
        P("fsdp", None),
        P(("task", "fsdp"), None),
        P("task", None),
        P(("task", "view"), "fsdp", None),
        P(("task", "view"), "fsdp", None),
        P(("task", "view"), "fsdp", None),
        P(("task", "view"), "fsdp", None),
    )
    out_specs = (P(("task", "fsdp"), None), P("task", None), P(("task", "view"), "fsdp", None))
    local = fused_body if (mesh.shape["fsdp"], mesh.shape["view"]) == (8, 2) else body
    return jax.shard_map(local, mesh=mesh, in_specs=in_specs, out_specs=out_specs, check_vma=False)
```
